256 devices in a mesh: ctx: 32 (over y, z), tp: 8 (over x, core).
Axes of the slice: x: 4, y: 4, z: 8, core: 2. Of those that a mesh axis runs over, the one named last changes fastest.
Arguments:
- queries: bfloat16 [12288, 8192], P('ctx', 'tp'), may hold values from -96 to 96
- keys: bfloat16 [12288, 1024], P('ctx', 'tp'), may hold values from -6 to 6
- values: bfloat16 [12288, 1024], P('ctx', 'tp'), may hold values from -6 to 6
- doc_lengths: int32 [24], replicated, may hold values from 1 to 6912, 12288 in all
- out_weight: bfloat16 [8192, 5120], P('tp'), may hold values from -0.0625 to 0.0625
Outputs:
- projected: bfloat16 [12288, 5120], P('ctx', 'tp')
The draws below stay inside these ranges and needn't reach their ends.
Inputs may be any that keep to these rules, and one draw needn't show every extreme that they name: `doc_lengths`: positive lengths of the 24 documents in order; they sum to 12288 and the longest is exactly 6912.
All inputs are finite; a program needn't handle non-finite values.
Results may differ from the reference program's by a relative error of at most 0.017.
Values may be sent and summed in bfloat16 or wider, within the bound.
A program may use at most 64 MiB of HBM per device.

```python
import math
import jax
import jax.numpy as jnp
import numpy as np
from jax import lax

D = 5120
QUERY_HEADS = 64
KEY_VALUE_HEADS = 8
HEAD_SIZE = 128
DOCS = 24
PACKED_TOKENS = 12288
MOST = 6912
N_TP = 8


def paired_keys(key):
    starting_keys = jax.random.normal(jax.random.fold_in(key, 11), (PACKED_TOKENS, KEY_VALUE_HEADS * HEAD_SIZE), jnp.float32)
    row_ids = jnp.arange(PACKED_TOKENS)
    marked = ((row_ids + 1) % 61 == 7)[:, None]
    return jnp.where(marked, starting_keys, starting_keys)


def draw_keys(key, part):
    return jnp.clip(paired_keys(key), -6.0, 6.0).astype(jnp.bfloat16)


def draw_queries(key, part):
    own_key = jax.random.fold_in(key, 3)
    base_queries = jax.random.normal(own_key, (PACKED_TOKENS, QUERY_HEADS * HEAD_SIZE), jnp.float32)
    row_ids = jnp.arange(PACKED_TOKENS)
    marked = (row_ids % 61 == 7)[:, None]
    aligned = jnp.where(marked, base_queries, base_queries)
    return jnp.clip(aligned, -96.0, 96.0).astype(jnp.bfloat16)


def level_of(key, dims, split, low, largest):
    def one(axis_at, shards_of):
        draws = jax.random.uniform(jax.random.fold_in(jax.random.fold_in(key, 6), axis_at), (shards_of,), jnp.float32, low / len(split), largest / len(split))
        return jnp.repeat(jnp.exp(draws), dims[axis_at] // shards_of).reshape((-1,) + (1,) * (len(dims) - axis_at - 1))

    loudness = one(*split[0])
    for cut in split[1:]:
        loudness = loudness * one(*cut)
    return loudness


def length_profile(number_of, total, reach, skew):
    loads = [(1 << 20) // math.isqrt(standing ** skew) + 1 for standing in range(2, number_of + 1)]
    spare, counts = total - reach - (number_of - 1), [1] * (number_of - 1)
    while spare > 0:
        free = [i for i in range(number_of - 1) if counts[i] < reach]
        mass, left = sum([loads[i] for i in free]), spare
        for i in free:
            addition = min(reach - counts[i], max(1, left * loads[i] // mass), spare)
            counts[i] = counts[i] + addition
            spare = spare - addition
    return np.array([reach] + counts)


def uneven_parts(key, number_of, total, limit, skew):
    if number_of == 2:
        one = jax.random.randint(key, (), max(1, total - limit), min(limit, total - 1) + 1)
        return jnp.stack([one, total - one])
    tallies = jnp.asarray(length_profile(number_of, total, limit, skew), jnp.int32)
    couples = (number_of - 1) // 2
    donor, sink = tallies[1:1 + 2 * couples:2], tallies[2:2 + 2 * couples:2]
    margin = jnp.minimum(donor - 1, limit - sink)
    moved = jax.random.randint(jax.random.fold_in(key, 1), (couples,), 0, 1 << 20) % (margin + 1)
    tallies = tallies.at[1:1 + 2 * couples:2].set(donor - moved).at[2:2 + 2 * couples:2].set(sink + moved)
    return tallies[jax.random.permutation(jax.random.fold_in(key, 2), number_of)]


def normal_values(rng, shape, spread, reach, pieces=(), held_as=jnp.bfloat16):
    gain = level_of(rng, shape, pieces, -0.22, 0.18) if pieces else 1.0
    result = jax.random.normal(rng, shape, jnp.float32) * spread * gain
    return jnp.minimum(jnp.maximum(result, -reach), reach).astype(held_as)


def setup_inputs(seed: int = 0) -> dict:
    streams_of = jax.random.split(jax.random.key(seed), 6)
    queries = draw_queries(jax.random.fold_in(streams_of[5], 71), 0)
    keys = draw_keys(jax.random.fold_in(streams_of[5], 71), 0)
    values = normal_values(streams_of[2], (PACKED_TOKENS, KEY_VALUE_HEADS * HEAD_SIZE), 1.0, 6.0, ((0, 32), (1, 8)))
    doc_lengths = uneven_parts(streams_of[3], DOCS, PACKED_TOKENS, MOST, 2).astype(jnp.int32)
    out_weight = normal_values(streams_of[4], (QUERY_HEADS * HEAD_SIZE, D), (QUERY_HEADS * HEAD_SIZE) ** -0.5, 0.0625, ((0, 8),))
    return {"queries": queries, "keys": keys, "values": values, "doc_lengths": doc_lengths, "out_weight": out_weight}


def doc_begin(doc_lengths, positions):
    doc_ends = jnp.cumsum(doc_lengths).astype(jnp.int32)
    doc_firsts = (doc_ends - doc_lengths).astype(jnp.int32)
    covered = doc_firsts[None, :] <= positions[:, None]
    return lax.optimization_barrier(jnp.max(jnp.where(covered, doc_firsts[None, :], 0), axis=1)).astype(jnp.int32)

def reference(queries, keys, values, doc_lengths, out_weight):
    group_length = QUERY_HEADS // KEY_VALUE_HEADS
    query_span = 256 if PACKED_TOKENS % 256 == 0 else PACKED_TOKENS
    key_window = min(PACKED_TOKENS, MOST + query_span)
    scale_factor = 1.0 / math.sqrt(HEAD_SIZE)
    query_head_rows = queries.reshape(PACKED_TOKENS, KEY_VALUE_HEADS, group_length, HEAD_SIZE)
    key_head_rows = keys.reshape(PACKED_TOKENS, KEY_VALUE_HEADS, HEAD_SIZE)
    value_head_rows = values.reshape(PACKED_TOKENS, KEY_VALUE_HEADS, HEAD_SIZE)

    def one_block(block_first):
        query_block = lax.dynamic_slice_in_dim(query_head_rows, block_first, query_span, 0).astype(jnp.float32)
        key_first = jnp.clip(block_first + query_span - key_window, 0, PACKED_TOKENS - key_window).astype(jnp.int32)
        key_block = lax.dynamic_slice_in_dim(key_head_rows, key_first, key_window, 0).astype(jnp.float32)
        value_block = lax.dynamic_slice_in_dim(value_head_rows, key_first, key_window, 0).astype(jnp.float32)
        query_pos = block_first + jnp.arange(query_span, dtype=jnp.int32)
        key_pos = key_first + jnp.arange(key_window, dtype=jnp.int32)
        query_doc = doc_begin(doc_lengths, query_pos)
        visible = (key_pos[None, :] >= query_doc[:, None]) & (key_pos[None, :] <= query_pos[:, None])
        visible = visible[:, None, None, :]
        scores = jnp.einsum('qgjd,kgd->qgjk', query_block, key_block) * scale_factor
        highest = lax.optimization_barrier(jnp.max(jnp.where(visible, scores, -jnp.inf), axis=-1, keepdims=True))
        weights = jnp.where(visible, jnp.exp(scores - highest), 0.0)
        weight_total = lax.optimization_barrier(jnp.sum(weights, axis=-1))
        rounded = lax.optimization_barrier(weights.astype(jnp.bfloat16)).astype(jnp.float32)
        attended = jnp.einsum('qgjk,kgd->qgjd', rounded, value_block) / weight_total[..., None]
        return attended.astype(jnp.bfloat16).reshape(query_span, QUERY_HEADS * HEAD_SIZE)
    block_firsts = jnp.arange(PACKED_TOKENS // query_span, dtype=jnp.int32) * query_span
    attended = lax.map(one_block, block_firsts).reshape(PACKED_TOKENS, QUERY_HEADS * HEAD_SIZE)
    group_width = QUERY_HEADS * HEAD_SIZE // N_TP
    projected = jnp.zeros((PACKED_TOKENS, D), jnp.float32)
    for group_index in range(N_TP):
        first_col = group_index * group_width
        partial_value = jnp.dot(attended[:, first_col:first_col + group_width], out_weight[first_col:first_col + group_width], preferred_element_type=jnp.float32)
        projected = projected + lax.optimization_barrier(partial_value.astype(jnp.bfloat16)).astype(jnp.float32)
    return projected.astype(jnp.bfloat16)
```

```python
import functools
import math

import jax
import jax.numpy as jnp
from jax import lax
from jax.experimental import pallas as pl
from jax.experimental.pallas import tpu as pltpu
from jax.sharding import PartitionSpec as P

MESH = pl.DeviceIdType.MESH
HEAD = 128
GROUP = 8
ROWS = 384
CHUNK = 512
NY, NZ, NX, NK = 4, 8, 4, 2
WIDE = 640
COLS = GROUP * ROWS
SCALE = math.log2(math.e) / math.sqrt(HEAD)
BIG = 262144.0
LOW = -1e30

ORDER = ((0,), (8,), (16,), (1, 7), (9, 17), (2, 15), (6, 18), (10, 14), (3, 5), (11, 13), (4, 12))
TICKS = (
    (
        (1, 1, 1, 0, 1), (1, 3, 0, 3, 0), (1, 1, 0, 0, 1), (1, 2, 1, 1, 0), (1, 2, 0, 1, 0), (1, 0, 1, 0, 7),
        (1, 0, 0, 0, 7),
    ),
    (
        (0, 0, 3, 0), (1, 3, 0, 2, 0), (0, 1, 0, 1), (0, 1, 1, 0), (0, 1, 0, 7), (1, 1, 1, 0, 2),
        (1, 1, 1, 1, 1), (1, 0, 1, 1, 7), (1, 0, 1, 0, 6), (1, 2, 1, 2, 0), (0, 0, 0, 1), (0, 0, 1, 0),
        (0, 0, 0, 7), (1, 3, 0, 3, 7), (1, 2, 0, 1, 1), (1, 1, 0, 0, 2), (1, 3, 0, 3, 1), (1, 0, 0, 0, 6),
        (1, 2, 0, 1, 7),
    ),
    (
        (0, 0, 2, 0), (0, 0, 3, 7), (0, 1, 0, 2), (0, 1, 1, 7), (0, 1, 2, 0), (1, 2, 1, 2, 7),
        (1, 3, 0, 2, 7), (1, 0, 1, 1, 6), (1, 1, 1, 0, 3),
    ),
    (
        (0, 0, 3, 1), (0, 0, 1, 1), (1, 3, 0, 2, 1), (0, 1, 1, 1), (0, 1, 0, 6), (0, 0, 1, 7),
        (1, 2, 1, 2, 1), (1, 1, 1, 1, 2), (1, 0, 1, 0, 5),
    ),
    (
        (0, 0, 2, 7), (0, 0, 0, 2), (0, 0, 0, 6), (0, 0, 2, 1), (0, 1, 2, 7), (1, 1, 0, 0, 3),
        (1, 0, 1, 2, 6), (1, 2, 0, 1, 6), (1, 2, 0, 1, 2), (1, 1, 0, 2, 2), (1, 0, 0, 0, 5), (1, 3, 0, 3, 6),
        (3,),
    ),
    (
        (0, 1, 1, 6), (0, 1, 0, 3), (0, 1, 2, 1), (0, 0, 3, 6), (0, 1, 1, 2), (0, 1, 0, 5), (2,),
        (0, 0, 1, 6), (1, 1, 1, 2, 2), (1, 2, 1, 1, 3), (1, 3, 0, 2, 6), (1, 2, 1, 1, 5), (1, 1, 1, 0, 4),
    ),
    (
        (0, 0, 0, 3), (0, 0, 1, 2), (0, 1, 2, 6), (0, 0, 2, 2), (0, 0, 2, 6), (1, 2, 0, 1, 3),
        (1, 1, 0, 0, 4), (1, 1, 0, 2, 3), (1, 0, 1, 2, 5),
    ),
    (
        (0, 0, 0, 5), (0, 1, 1, 3), (0, 1, 2, 2), (0, 1, 1, 5), (1, 0, 1, 1, 4), (1, 2, 0, 1, 5),
        (1, 3, 0, 3, 5), (1, 2, 1, 2, 3),
    ),
    (
        (0, 1, 2, 5), (0, 1, 0, 4), (0, 0, 1, 3), (0, 0, 0, 4), (0, 0, 1, 5), (0, 0, 3, 5), (0, 0, 2, 3),
        (1, 0, 1, 2, 4), (1, 3, 0, 2, 5), (1, 1, 0, 2, 4), (1, 2, 0, 1, 4),
    ),
    (
        (0, 1, 1, 4), (0, 1, 2, 3), (0, 0, 2, 5), (0, 0, 2, 4), (0, 0, 1, 4),
    ),
    (
        (0, 1, 2, 4),
    ),
)
MESSAGES = tuple(item[1:] for tick in TICKS for item in tick if item[0] == 1)


def pick(index, numbers):
    value = jnp.int32(numbers[0])
    for at, number in enumerate(numbers[1:], 1):
        value = jnp.where(index == at, jnp.int32(number), value)
    return value


def kernel(
    q_ref, k_ref, v_ref, len_ref, w_ref, out_ref,
    qt, kv, acc, top, qpos, firsts, lasts, wts, att, far, near_r, near_l, mid_l, mid_r, in_l, in_r,
    kv_send, kv_recv, sp_send, sp_recv, w_local, w_send, w_recv, a_send, a_recv, x_send, x_recv,
):
    ctx, tp = lax.axis_index("ctx"), lax.axis_index("tp")
    y, z = ctx // NZ, lax.rem(ctx, NZ)
    x, core = tp // NK, lax.rem(tp, NK)
    z_next = (y * NZ + lax.rem(z + 1, NZ), tp)
    z_back = (y * NZ + lax.rem(z + NZ - 1, NZ), tp)
    y_next = (lax.rem(y + 1, NY) * NZ + z, tp)
    y_back = (lax.rem(y + NY - 1, NY) * NZ + z, tp)
    x_next = (ctx, lax.rem(x + 1, NX) * NK + core)
    x_back = (ctx, lax.rem(x + NX - 1, NX) * NK + core)
    other = (ctx, x * NK + 1 - core)
    links = (z_next, z_back, y_next, y_back)
    shift = ((0, 1), (0, -1), (-1, 0), (1, 0))

    kv[3, 6:8, 1:3] = jnp.zeros((2, 2, 2 * HEAD, HEAD), jnp.bfloat16)
    barrier = pltpu.get_barrier_semaphore()
    for device in links + (x_next, x_back, other):
        pl.semaphore_signal(barrier, inc=1, device_id=device, device_id_type=MESH)

    values_t = v_ref[...].astype(jnp.float32).T.astype(jnp.bfloat16)
    for c in range(3):
        kv[0, z, c, 0:HEAD, :] = k_ref[c * HEAD:(c + 1) * HEAD, :]
        kv[0, z, c, HEAD:, :] = values_t[:, c * HEAD:(c + 1) * HEAD]

    def message(link, part, row, column):
        piece = pl.ds(0, 1) if part == 0 else pl.ds(1, 2)
        dy, dz = shift[link]
        held = (row + dy) % NY
        col = lax.rem(z + (column + dz) + 2 * NZ, NZ)
        return pltpu.make_async_remote_copy(
            src_ref=kv.at[held, col, piece],
            dst_ref=kv.at[row, col, piece],
            send_sem=kv_send.at[part, row, column],
            recv_sem=kv_recv.at[part, row, column],
            device_id=links[link],
            device_id_type=MESH,
        )

    def arrival(part, row, column):
        piece = pl.ds(0, 1) if part == 0 else pl.ds(1, 2)
        slot = kv.at[row, lax.rem(z + column, NZ), piece]
        return pltpu.make_async_remote_copy(
            src_ref=slot,
            dst_ref=slot,
            send_sem=kv_send.at[part, row, column],
            recv_sem=kv_recv.at[part, row, column],
            device_id=z_next,
            device_id_type=MESH,
        )

    def special(at):
        return pltpu.make_async_remote_copy(
            src_ref=kv.at[0, 6 + at, pl.ds(1, 2)],
            dst_ref=kv.at[3, 6 + at, pl.ds(1, 2)],
            send_sem=sp_send.at[at],
            recv_sem=sp_recv.at[at],
            device_id=y_back,
            device_id_type=MESH,
        )

    sends_special = (y == 0) & (z < 2)
    takes_special = (y == NY - 1) & (z < 2)

    def act(item):
        if item[0] == 0:
            arrival(*item[1:]).wait_recv()
        elif item[0] == 1:
            message(*item[1:]).start()
        elif item[0] == 2:
            @pl.when(sends_special)
            def _():
                for at in range(2):
                    special(at).start()
        else:
            @pl.when(takes_special)
            def _():
                for at in range(2):
                    special(at).wait_recv()

    pl.semaphore_wait(barrier, 7)
    for item in TICKS[0]:
        act(item)

    def weight_columns(xx, half):
        return pl.ds(pl.multiple_of(xx * (2 * WIDE) + half * WIDE, HEAD), WIDE)

    def weight_keep(xx):
        return pltpu.make_async_copy(w_ref.at[:, weight_columns(xx, core)], wts.at[core, xx], w_local.at[xx])

    def weight_give(xx):
        return pltpu.make_async_remote_copy(
            src_ref=w_ref.at[:, weight_columns(xx, 1 - core)],
            dst_ref=wts.at[core, xx],
            send_sem=w_send.at[xx],
            recv_sem=w_recv.at[xx],
            device_id=other,
            device_id_type=MESH,
        )

    for xx in range(NX):
        weight_keep(xx).start()
        weight_give(xx).start()

    lane = lax.broadcasted_iota(jnp.int32, (8, HEAD), 1)
    sub = lax.broadcasted_iota(jnp.int32, (HEAD, ROWS), 0)
    first_l = jnp.where(lane == HEAD - 1, -(1 << 30), 0)
    last_l = jnp.zeros_like(lane)
    first_s, last_s = jnp.zeros_like(sub), jnp.zeros_like(sub)
    begin = jnp.int32(0)
    for d in range(24):
        end = begin + len_ref[d]
        first_l, last_l = jnp.where(lane == d, begin, first_l), jnp.where(lane == d, end, last_l)
        first_s, last_s = jnp.where(sub == d, begin, first_s), jnp.where(sub == d, end, last_s)
        begin = end
    firsts[...] = first_l
    lasts[...] = last_l
    own = ctx * ROWS + lax.broadcasted_iota(jnp.int32, (HEAD, ROWS), 1)
    apart = jnp.where((own >= first_s) & (own < last_s), 0.0, -BIG).astype(jnp.bfloat16)
    for h in range(GROUP):
        span = slice(h * ROWS, (h + 1) * ROWS)
        qt[0:HEAD, span] = q_ref[:, h * HEAD:(h + 1) * HEAD].astype(jnp.float32).T.astype(jnp.bfloat16)
        qt[HEAD:, span] = apart
        qpos[:, span] = own[0:8]
    top[...] = jnp.full_like(top, LOW)
    acc[...] = jnp.zeros_like(acc)

    def block(delta):
        row = (delta - z + NZ - 1) // NZ
        col = lax.rem(z - delta + 3 * NZ, NZ)
        held = kv[row, col]
        pos = (ctx - delta) * ROWS + lax.broadcasted_iota(jnp.int32, (ROWS, HEAD), 0)
        same = jnp.where((pos >= firsts[0:1, :]) & (pos < lasts[0:1, :]), 1.0, 0.0).astype(jnp.bfloat16)
        keys = jnp.concatenate([held[c, 0:HEAD] for c in range(3)], axis=0)
        vals = jnp.concatenate([held[c, HEAD:] for c in range(3)], axis=1)
        return jnp.concatenate([keys, same], axis=1), vals

    def attend(deltas, causal):
        parts = [block(delta) for delta in deltas]
        keys = jnp.concatenate([part[0] for part in parts], axis=0)
        vals = jnp.concatenate([part[1] for part in parts], axis=1)
        count = keys.shape[0]
        vals = jnp.concatenate([vals, jnp.ones((16, count), jnp.bfloat16)], axis=0)

        def score(j):
            span = slice(j * CHUNK, (j + 1) * CHUNK)
            got = jnp.dot(keys, qt[:, span], preferred_element_type=jnp.float32)
            if causal:
                pos = (ctx - deltas[0]) * ROWS + lax.broadcasted_iota(jnp.int32, (count, CHUNK), 0)
                got = jnp.where(pos <= qpos[0:1, span], got, -BIG)
            return got

        def soften(j, got):
            span = slice(j * CHUNK, (j + 1) * CHUNK)
            old = top[0:1, span]
            new = jnp.maximum(old, jnp.max(got, axis=0, keepdims=True))
            top[0:1, span] = new
            return jnp.exp2((got - new) * SCALE).astype(jnp.bfloat16), jnp.exp2((old - new) * SCALE)

        def gather(j, weights, fade):
            span = slice(j * CHUNK, (j + 1) * CHUNK)
            acc[:, span] = acc[:, span] * fade + jnp.dot(vals, weights, preferred_element_type=jnp.float32)

        steps = COLS // CHUNK
        got, held = score(0), None
        for j in range(steps):
            ahead = score(j + 1) if j + 1 < steps else None
            soft = soften(j, got)
            if held is not None:
                gather(j - 1, *held)
            got, held = ahead, soft
        gather(steps - 1, *held)

    def step(i, carry):
        for at in range(1, len(ORDER)):
            @pl.when(i == at)
            def _(at=at):
                for item in TICKS[at]:
                    act(item)
        one = pick(i, [min(group) for group in ORDER])
        two = pick(i, [max(group) for group in ORDER])

        @pl.when((one == two) & (ctx >= one))
        def _():
            attend((one,), True)

        @pl.when((one != two) & (ctx >= one))
        def _():
            attend((one, two), False)

        return carry

    lax.fori_loop(0, len(ORDER), step, 0)

    for h in range(GROUP):
        span = slice(h * ROWS, (h + 1) * ROWS)
        rows = acc[0:HEAD, span] / acc[HEAD:HEAD + 1, span]
        att[core, :, h * HEAD:(h + 1) * HEAD] = rows.T.astype(jnp.bfloat16)
    swap = pltpu.make_async_remote_copy(
        src_ref=att.at[core], dst_ref=att.at[core], send_sem=a_send, recv_sem=a_recv, device_id=other, device_id_type=MESH,
    )
    swap.start()
    for xx in range(NX):
        weight_keep(xx).wait()
        weight_give(xx).wait()
    swap.wait()

    half = ROWS // 2
    lower, upper = pl.ds(0, half), pl.ds(half, half)

    def project(xx):
        total = jnp.dot(att[0], wts[0, xx], preferred_element_type=jnp.float32)
        return total + jnp.dot(att[1], wts[1, xx], preferred_element_type=jnp.float32)

    def along(at, src, dst, device):
        return pltpu.make_async_remote_copy(
            src_ref=src, dst_ref=dst, send_sem=x_send.at[at], recv_sem=x_recv.at[at], device_id=device, device_id_type=MESH,
        )

    far_up = along(0, far.at[lower], mid_l, x_next)
    far_down = along(1, far.at[upper], mid_r, x_back)
    up_a = along(2, near_r.at[upper], in_l.at[upper], x_next)
    down_a = along(3, near_l.at[lower], in_r.at[lower], x_back)
    up_b = along(4, near_r.at[lower], in_l.at[lower], x_next)
    down_b = along(5, near_l.at[upper], in_r.at[upper], x_back)

    far[...] = project(lax.rem(x + 2, NX)).astype(jnp.bfloat16)
    far_up.start()
    far_down.start()
    near_r[...] = project(lax.rem(x + 1, NX)).astype(jnp.bfloat16)
    up_a.start()
    near_l[...] = project(lax.rem(x + NX - 1, NX)).astype(jnp.bfloat16)
    down_a.start()
    far_up.wait_recv()
    near_r[0:half] = (near_r[0:half].astype(jnp.float32) + mid_l[...].astype(jnp.float32)).astype(jnp.bfloat16)
    up_b.start()
    far_down.wait_recv()
    near_l[half:] = (near_l[half:].astype(jnp.float32) + mid_r[...].astype(jnp.float32)).astype(jnp.bfloat16)
    down_b.start()
    mine = project(x)
    for copy in (up_a, down_a, up_b, down_b):
        copy.wait_recv()
    out_ref[...] = (mine + in_l[...].astype(jnp.float32) + in_r[...].astype(jnp.float32)).astype(jnp.bfloat16)
    for copy in (far_up, far_down, up_a, down_a, up_b, down_b):
        copy.wait_send()
    for item in MESSAGES:
        message(*item).wait_send()

    @pl.when(sends_special)
    def _():
        for at in range(2):
            special(at).wait_send()


def local(queries, keys, values, doc_lengths, out_weight):
    vmem = pl.BlockSpec(memory_space=pltpu.VMEM)
    bf16, f32 = jnp.bfloat16, jnp.float32
    dma = pltpu.SemaphoreType.DMA
    return pl.pallas_call(
        kernel,
        out_shape=jax.ShapeDtypeStruct((ROWS, WIDE), bf16),
        in_specs=[vmem, vmem, vmem, pl.BlockSpec(memory_space=pltpu.SMEM), pl.BlockSpec(memory_space=pl.ANY)],
        out_specs=vmem,
        scratch_shapes=[
            pltpu.VMEM((2 * HEAD, COLS), bf16),
            pltpu.VMEM((NY, NZ, 3, 2 * HEAD, HEAD), bf16),
            pltpu.VMEM((HEAD + 16, COLS), f32),
            pltpu.VMEM((8, COLS), f32),
            pltpu.VMEM((8, COLS), jnp.int32),
            pltpu.VMEM((8, HEAD), jnp.int32),
            pltpu.VMEM((8, HEAD), jnp.int32),
            pltpu.VMEM((NK, NX, GROUP * HEAD, WIDE), bf16),
            pltpu.VMEM((NK, ROWS, GROUP * HEAD), bf16),
            pltpu.VMEM((ROWS, WIDE), bf16),
            pltpu.VMEM((ROWS, WIDE), bf16),
            pltpu.VMEM((ROWS, WIDE), bf16),
            pltpu.VMEM((ROWS // 2, WIDE), bf16),
            pltpu.VMEM((ROWS // 2, WIDE), bf16),
            pltpu.VMEM((ROWS, WIDE), bf16),
            pltpu.VMEM((ROWS, WIDE), bf16),
            dma((2, NY, NZ)),
            dma((2, NY, NZ)),
            dma((2,)),
            dma((2,)),
            dma((NX,)),
            dma((NX,)),
            dma((NX,)),
            dma,
            dma,
            dma((6,)),
            dma((6,)),
        ],
        compiler_params=pltpu.CompilerParams(
            collective_id=0, has_side_effects=True, vmem_limit_bytes=60 << 20
        ),
    )(queries, keys, values, doc_lengths, out_weight)


def solution(mesh):
    in_specs = (P("ctx", "tp"), P("ctx", "tp"), P("ctx", "tp"), P(), P("tp", None))
    out_specs = P("ctx", "tp")
    return jax.shard_map(local, mesh=mesh, in_specs=in_specs, out_specs=out_specs, check_vma=False)
```

```python
import functools
import math

import jax
import jax.numpy as jnp
from jax import lax
from jax.experimental import pallas as pl
from jax.experimental.pallas import tpu as pltpu
from jax.sharding import PartitionSpec as P

MESH = pl.DeviceIdType.MESH
HEAD = 128
GROUP = 8
ROWS = 384
CHUNK = 512
NY, NZ, NX, NK = 4, 8, 4, 2
WIDE = 640
COLS = GROUP * ROWS
TILES = 3
TILE = ROWS // TILES
SPAN = GROUP * TILE
SCALE = math.log2(math.e) / math.sqrt(HEAD)
BIG = 262144.0
LOW = -1e30

ORDER = ((0,), (8,), (16,), (1, 7), (9, 17), (2, 15), (6, 18), (10, 14), (3, 5))
LAST = (4, 11, 12, 13)
TICKS = (
    (
        (1, 1, 1, 0, 1), (1, 3, 0, 3, 0), (1, 1, 0, 0, 1), (1, 2, 1, 1, 0), (1, 2, 0, 1, 0), (1, 0, 1, 0, 7),
        (1, 0, 0, 0, 7),
    ),
    (
        (0, 0, 3, 0), (1, 3, 0, 2, 0), (0, 1, 0, 1), (0, 1, 1, 0), (0, 1, 0, 7), (1, 1, 1, 0, 2),
        (1, 1, 1, 1, 1), (1, 0, 1, 1, 7), (1, 0, 1, 0, 6), (1, 2, 1, 2, 0), (0, 0, 0, 1), (0, 0, 1, 0),
        (0, 0, 0, 7), (1, 3, 0, 3, 7), (1, 2, 0, 1, 1), (1, 1, 0, 0, 2), (1, 3, 0, 3, 1), (1, 0, 0, 0, 6),
        (1, 2, 0, 1, 7),
    ),
    (
        (0, 0, 2, 0), (0, 0, 3, 7), (0, 1, 0, 2), (0, 1, 1, 7), (0, 1, 2, 0), (1, 2, 1, 2, 7),
        (1, 3, 0, 2, 7), (1, 0, 1, 1, 6), (1, 1, 1, 0, 3),
    ),
    (
        (0, 0, 3, 1), (0, 0, 1, 1), (1, 3, 0, 2, 1), (0, 1, 1, 1), (0, 1, 0, 6), (0, 0, 1, 7),
        (1, 2, 1, 2, 1), (1, 1, 1, 1, 2), (1, 0, 1, 0, 5),
    ),
    (
        (0, 0, 2, 7), (0, 0, 0, 2), (0, 0, 0, 6), (0, 0, 2, 1), (0, 1, 2, 7), (1, 1, 0, 0, 3),
        (1, 0, 1, 2, 6), (1, 2, 0, 1, 6), (1, 2, 0, 1, 2), (1, 1, 0, 2, 2), (1, 0, 0, 0, 5), (1, 3, 0, 3, 6),
        (3,),
    ),
    (
        (0, 1, 1, 6), (0, 1, 0, 3), (0, 1, 2, 1), (0, 0, 3, 6), (0, 1, 1, 2), (0, 1, 0, 5), (2,),
        (0, 0, 1, 6), (1, 1, 1, 2, 2), (1, 2, 1, 1, 3), (1, 3, 0, 2, 6), (1, 2, 1, 1, 5), (1, 1, 1, 0, 4),
    ),
    (
        (0, 0, 0, 3), (0, 0, 1, 2), (0, 1, 2, 6), (0, 0, 2, 2), (0, 0, 2, 6), (1, 2, 0, 1, 3),
        (1, 1, 0, 0, 4), (1, 1, 0, 2, 3), (1, 0, 1, 2, 5),
    ),
    (
        (0, 0, 0, 5), (0, 1, 1, 3), (0, 1, 2, 2), (0, 1, 1, 5), (1, 0, 1, 1, 4), (1, 2, 0, 1, 5),
        (1, 3, 0, 3, 5), (1, 2, 1, 2, 3),
    ),
    (
        (0, 1, 2, 5), (0, 1, 0, 4), (0, 0, 1, 3), (0, 0, 0, 4), (0, 0, 1, 5), (0, 0, 3, 5), (0, 0, 2, 3),
        (1, 0, 1, 2, 4), (1, 3, 0, 2, 5), (1, 1, 0, 2, 4), (1, 2, 0, 1, 4),
    ),
    (
        (0, 1, 1, 4), (0, 1, 2, 3), (0, 0, 2, 5), (0, 0, 2, 4), (0, 0, 1, 4), (0, 1, 2, 4),
    ),
)
MESSAGES = tuple(item[1:] for tick in TICKS for item in tick if item[0] == 1)


def pick(index, numbers):
    value = jnp.int32(numbers[0])
    for at, number in enumerate(numbers[1:], 1):
        value = jnp.where(index == at, jnp.int32(number), value)
    return value


def kernel(
    q_ref, k_ref, v_ref, len_ref, w_ref, out_ref,
    qt, kv, acc, top, qpos, firsts, lasts, wts, att, far, near_r, near_l, mid_l, mid_r, in_l, in_r, mine,
    kv_send, kv_recv, sp_send, sp_recv, w_local, w_send, w_recv, a_send, a_recv, x_send, x_recv,
):
    ctx, tp = lax.axis_index("ctx"), lax.axis_index("tp")
    y, z = ctx // NZ, lax.rem(ctx, NZ)
    x, core = tp // NK, lax.rem(tp, NK)
    z_next = (y * NZ + lax.rem(z + 1, NZ), tp)
    z_back = (y * NZ + lax.rem(z + NZ - 1, NZ), tp)
    y_next = (lax.rem(y + 1, NY) * NZ + z, tp)
    y_back = (lax.rem(y + NY - 1, NY) * NZ + z, tp)
    x_next = (ctx, lax.rem(x + 1, NX) * NK + core)
    x_back = (ctx, lax.rem(x + NX - 1, NX) * NK + core)
    other = (ctx, x * NK + 1 - core)
    links = (z_next, z_back, y_next, y_back)
    shift = ((0, 1), (0, -1), (-1, 0), (1, 0))

    kv[3, 6:8, 1:3] = jnp.zeros((2, 2, 2 * HEAD, HEAD), jnp.bfloat16)
    barrier = pltpu.get_barrier_semaphore()
    for device in links + (x_next, x_back, other):
        pl.semaphore_signal(barrier, inc=1, device_id=device, device_id_type=MESH)

    values_t = v_ref[...].astype(jnp.float32).T.astype(jnp.bfloat16)
    for c in range(3):
        kv[0, z, c, 0:HEAD, :] = k_ref[c * HEAD:(c + 1) * HEAD, :]
        kv[0, z, c, HEAD:, :] = values_t[:, c * HEAD:(c + 1) * HEAD]

    def message(link, part, row, column):
        piece = pl.ds(0, 1) if part == 0 else pl.ds(1, 2)
        dy, dz = shift[link]
        held = (row + dy) % NY
        col = lax.rem(z + (column + dz) + 2 * NZ, NZ)
        return pltpu.make_async_remote_copy(
            src_ref=kv.at[held, col, piece],
            dst_ref=kv.at[row, col, piece],
            send_sem=kv_send.at[part, row, column],
            recv_sem=kv_recv.at[part, row, column],
            device_id=links[link],
            device_id_type=MESH,
        )

    def arrival(part, row, column):
        piece = pl.ds(0, 1) if part == 0 else pl.ds(1, 2)
        slot = kv.at[row, lax.rem(z + column, NZ), piece]
        return pltpu.make_async_remote_copy(
            src_ref=slot,
            dst_ref=slot,
            send_sem=kv_send.at[part, row, column],
            recv_sem=kv_recv.at[part, row, column],
            device_id=z_next,
            device_id_type=MESH,
        )

    def special(at):
        return pltpu.make_async_remote_copy(
            src_ref=kv.at[0, 6 + at, pl.ds(1, 2)],
            dst_ref=kv.at[3, 6 + at, pl.ds(1, 2)],
            send_sem=sp_send.at[at],
            recv_sem=sp_recv.at[at],
            device_id=y_back,
            device_id_type=MESH,
        )

    sends_special = (y == 0) & (z < 2)
    takes_special = (y == NY - 1) & (z < 2)

    def act(item):
        if item[0] == 0:
            arrival(*item[1:]).wait_recv()
        elif item[0] == 1:
            message(*item[1:]).start()
        elif item[0] == 2:
            @pl.when(sends_special)
            def _():
                for at in range(2):
                    special(at).start()
        else:
            @pl.when(takes_special)
            def _():
                for at in range(2):
                    special(at).wait_recv()

    pl.semaphore_wait(barrier, 7)
    for item in TICKS[0]:
        act(item)

    def weight_columns(xx, half):
        return pl.ds(pl.multiple_of(xx * (2 * WIDE) + half * WIDE, HEAD), WIDE)

    def weight_keep(xx):
        return pltpu.make_async_copy(w_ref.at[:, weight_columns(xx, core)], wts.at[core, xx], w_local.at[xx])

    def weight_give(xx):
        return pltpu.make_async_remote_copy(
            src_ref=w_ref.at[:, weight_columns(xx, 1 - core)],
            dst_ref=wts.at[core, xx],
            send_sem=w_send.at[xx],
            recv_sem=w_recv.at[xx],
            device_id=other,
            device_id_type=MESH,
        )

    for xx in range(NX):
        weight_keep(xx).start()
        weight_give(xx).start()

    lane = lax.broadcasted_iota(jnp.int32, (8, HEAD), 1)
    sub = lax.broadcasted_iota(jnp.int32, (HEAD, ROWS), 0)
    first_l = jnp.where(lane == HEAD - 1, -(1 << 30), 0)
    last_l = jnp.zeros_like(lane)
    first_s, last_s = jnp.zeros_like(sub), jnp.zeros_like(sub)
    begin = jnp.int32(0)
    for d in range(24):
        end = begin + len_ref[d]
        first_l, last_l = jnp.where(lane == d, begin, first_l), jnp.where(lane == d, end, last_l)
        first_s, last_s = jnp.where(sub == d, begin, first_s), jnp.where(sub == d, end, last_s)
        begin = end
    firsts[...] = first_l
    lasts[...] = last_l
    own = ctx * ROWS + lax.broadcasted_iota(jnp.int32, (HEAD, ROWS), 1)
    apart = jnp.where((own >= first_s) & (own < last_s), 0.0, -BIG).astype(jnp.bfloat16)
    for h in range(GROUP):
        turned = q_ref[:, h * HEAD:(h + 1) * HEAD].astype(jnp.float32).T.astype(jnp.bfloat16)
        for t in range(TILES):
            span = slice(t * SPAN + h * TILE, t * SPAN + (h + 1) * TILE)
            rows = slice(t * TILE, (t + 1) * TILE)
            qt[0:HEAD, span] = turned[:, rows]
            qt[HEAD:, span] = apart[:, rows]
            qpos[:, span] = own[0:8, rows]
    top[...] = jnp.full_like(top, LOW)
    acc[...] = jnp.zeros_like(acc)

    def block(delta):
        row = (delta - z + NZ - 1) // NZ
        col = lax.rem(z - delta + 3 * NZ, NZ)
        held = kv[row, col]
        pos = (ctx - delta) * ROWS + lax.broadcasted_iota(jnp.int32, (ROWS, HEAD), 0)
        same = jnp.where((pos >= firsts[0:1, :]) & (pos < lasts[0:1, :]), 1.0, 0.0).astype(jnp.bfloat16)
        keys = jnp.concatenate([held[c, 0:HEAD] for c in range(3)], axis=0)
        vals = jnp.concatenate([held[c, HEAD:] for c in range(3)], axis=1)
        return jnp.concatenate([keys, same], axis=1), vals

    def attend(deltas, causal, base, steps):
        parts = [block(delta) for delta in deltas]
        keys = jnp.concatenate([part[0] for part in parts], axis=0)
        vals = jnp.concatenate([part[1] for part in parts], axis=1)
        count = keys.shape[0]
        vals = jnp.concatenate([vals, jnp.ones((16, count), jnp.bfloat16)], axis=0)

        def span_of(j):
            if isinstance(base, int):
                return slice(base + j * CHUNK, base + (j + 1) * CHUNK)
            return pl.ds(pl.multiple_of(base + j * CHUNK, CHUNK), CHUNK)

        def score(j):
            span = span_of(j)
            got = jnp.dot(keys, qt[:, span], preferred_element_type=jnp.float32)
            if causal:
                pos = (ctx - deltas[0]) * ROWS + lax.broadcasted_iota(jnp.int32, (count, CHUNK), 0)
                got = jnp.where(pos <= qpos[0:1, span], got, -BIG)
            return got

        def soften(j, got):
            span = span_of(j)
            old = top[0:1, span]
            new = jnp.maximum(old, jnp.max(got, axis=0, keepdims=True))
            top[0:1, span] = new
            return jnp.exp2((got - new) * SCALE).astype(jnp.bfloat16), jnp.exp2((old - new) * SCALE)

        def gather(j, weights, fade):
            span = span_of(j)
            acc[:, span] = acc[:, span] * fade + jnp.dot(vals, weights, preferred_element_type=jnp.float32)

        got, held = score(0), None
        for j in range(steps):
            ahead = score(j + 1) if j + 1 < steps else None
            soft = soften(j, got)
            if held is not None:
                gather(j - 1, *held)
            got, held = ahead, soft
        gather(steps - 1, *held)

    def step(i, carry):
        for at in range(1, len(ORDER)):
            @pl.when(i == at)
            def _(at=at):
                for item in TICKS[at]:
                    act(item)
        one = pick(i, [min(group) for group in ORDER])
        two = pick(i, [max(group) for group in ORDER])

        @pl.when((one == two) & (ctx >= one))
        def _():
            attend((one,), True, 0, COLS // CHUNK)

        @pl.when((one != two) & (ctx >= one))
        def _():
            attend((one, two), False, 0, COLS // CHUNK)

        return carry

    lax.fori_loop(0, len(ORDER), step, 0)

    for item in TICKS[len(ORDER)]:
        act(item)
    for xx in range(NX):
        weight_keep(xx).wait()
        weight_give(xx).wait()

    half = TILE // 2

    def swap(t):
        held = att.at[core, t]
        return pltpu.make_async_remote_copy(
            src_ref=held, dst_ref=held, send_sem=a_send.at[t], recv_sem=a_recv.at[t], device_id=other, device_id_type=MESH,
        )

    def along(t, at, src, dst, device):
        return pltpu.make_async_remote_copy(
            src_ref=src,
            dst_ref=dst,
            send_sem=x_send.at[t, at],
            recv_sem=x_recv.at[t, at],
            device_id=device,
            device_id_type=MESH,
        )

    lower, upper = pl.ds(0, half), pl.ds(half, half)

    def copies(t):
        return (
            along(t, 0, far.at[t, lower], mid_l.at[t], x_next),
            along(t, 1, far.at[t, upper], mid_r.at[t], x_back),
            along(t, 2, near_r.at[t, upper], in_l.at[t, upper], x_next),
            along(t, 3, near_l.at[t, lower], in_r.at[t, lower], x_back),
            along(t, 4, near_r.at[t, lower], in_l.at[t, lower], x_next),
            along(t, 5, near_l.at[t, upper], in_r.at[t, upper], x_back),
        )

    def pass_on(t):
        far_up, far_down, _, _, up, down = copies(t)
        far_up.wait_recv()
        near_r[t, 0:half] = (near_r[t, 0:half].astype(jnp.float32) + mid_l[t].astype(jnp.float32)).astype(jnp.bfloat16)
        up.start()
        far_down.wait_recv()
        near_l[t, half:] = (near_l[t, half:].astype(jnp.float32) + mid_r[t].astype(jnp.float32)).astype(jnp.bfloat16)
        down.start()

    def finish(t, carry):
        base = t * SPAN

        @pl.when(ctx >= min(LAST))
        def _():
            attend(LAST, False, base, SPAN // CHUNK)

        for h in range(GROUP):
            span = pl.ds(pl.multiple_of(base + h * TILE, TILE), TILE)
            rows = acc[0:HEAD, span] / acc[HEAD:HEAD + 1, span]
            att[core, t, :, h * HEAD:(h + 1) * HEAD] = rows.T.astype(jnp.bfloat16)
        swap(t).start()

        @pl.when(t > 0)
        def _():
            pass_on(t - 1)

        targets = [lax.rem(x + step, NX) for step in (2, 1, 3, 0)]
        sums = [jnp.dot(att[core, t], wts[core, xx], preferred_element_type=jnp.float32) for xx in targets]
        swap(t).wait()

        def whole(at):
            return sums[at] + jnp.dot(att[1 - core, t], wts[1 - core, targets[at]], preferred_element_type=jnp.float32)

        far_up, far_down, up, down, _, _ = copies(t)
        far[t] = whole(0).astype(jnp.bfloat16)
        far_up.start()
        far_down.start()
        near_r[t] = whole(1).astype(jnp.bfloat16)
        up.start()
        near_l[t] = whole(2).astype(jnp.bfloat16)
        down.start()
        mine[t] = whole(3)
        return carry

    lax.fori_loop(0, TILES, finish, 0)
    pass_on(TILES - 1)
    for t in range(TILES):
        for copy in copies(t)[2:]:
            copy.wait_recv()
        total = mine[t] + in_l[t].astype(jnp.float32) + in_r[t].astype(jnp.float32)
        out_ref[t * TILE:(t + 1) * TILE] = total.astype(jnp.bfloat16)
    for t in range(TILES):
        for copy in copies(t):
            copy.wait_send()
    for item in MESSAGES:
        message(*item).wait_send()

    @pl.when(sends_special)
    def _():
        for at in range(2):
            special(at).wait_send()


def local(queries, keys, values, doc_lengths, out_weight):
    vmem = pl.BlockSpec(memory_space=pltpu.VMEM)
    bf16, f32 = jnp.bfloat16, jnp.float32
    dma = pltpu.SemaphoreType.DMA
    return pl.pallas_call(
        kernel,
        out_shape=jax.ShapeDtypeStruct((ROWS, WIDE), bf16),
        in_specs=[vmem, vmem, vmem, pl.BlockSpec(memory_space=pltpu.SMEM), pl.BlockSpec(memory_space=pl.ANY)],
        out_specs=vmem,
        scratch_shapes=[
            pltpu.VMEM((2 * HEAD, COLS), bf16),
            pltpu.VMEM((NY, NZ, 3, 2 * HEAD, HEAD), bf16),
            pltpu.VMEM((HEAD + 16, COLS), f32),
            pltpu.VMEM((8, COLS), f32),
            pltpu.VMEM((8, COLS), jnp.int32),
            pltpu.VMEM((8, HEAD), jnp.int32),
            pltpu.VMEM((8, HEAD), jnp.int32),
            pltpu.VMEM((NK, NX, GROUP * HEAD, WIDE), bf16),
            pltpu.VMEM((NK, TILES, TILE, GROUP * HEAD), bf16),
            pltpu.VMEM((TILES, TILE, WIDE), bf16),
            pltpu.VMEM((TILES, TILE, WIDE), bf16),
            pltpu.VMEM((TILES, TILE, WIDE), bf16),
            pltpu.VMEM((TILES, TILE // 2, WIDE), bf16),
            pltpu.VMEM((TILES, TILE // 2, WIDE), bf16),
            pltpu.VMEM((TILES, TILE, WIDE), bf16),
            pltpu.VMEM((TILES, TILE, WIDE), bf16),
            pltpu.VMEM((TILES, TILE, WIDE), f32),
            dma((2, NY, NZ)),
            dma((2, NY, NZ)),
            dma((2,)),
            dma((2,)),
            dma((NX,)),
            dma((NX,)),
            dma((NX,)),
            dma((TILES,)),
            dma((TILES,)),
            dma((TILES, 6)),
            dma((TILES, 6)),
        ],
        compiler_params=pltpu.CompilerParams(
            collective_id=0, has_side_effects=True, vmem_limit_bytes=60 << 20
        ),
    )(queries, keys, values, doc_lengths, out_weight)


def solution(mesh):
    in_specs = (P("ctx", "tp"), P("ctx", "tp"), P("ctx", "tp"), P(), P("tp", None))
    out_specs = P("ctx", "tp")
    return jax.shard_map(local, mesh=mesh, in_specs=in_specs, out_specs=out_specs, check_vma=False)
```

```python
import functools
import math

import jax
import jax.numpy as jnp
from jax import lax
from jax.experimental import pallas as pl
from jax.experimental.pallas import tpu as pltpu
from jax.sharding import PartitionSpec as P

MESH = pl.DeviceIdType.MESH
HEAD = 128
GROUP = 8
ROWS = 384
CHUNK = 512
NY, NZ, NX, NK = 4, 8, 4, 2
WIDE = 640
COLS = GROUP * ROWS
TILES = 3
TILE = ROWS // TILES
SPAN = GROUP * TILE
SCALE = math.log2(math.e) / math.sqrt(HEAD)
BIG = 262144.0
LOW = -1e30

ORDER = ((0,), (8,), (16,), (1, 7), (6, 9), (15, 17), (2, 5), (10, 14), (13, 18))
LAST = (3, 4, 11, 12)
TICKS = (
    (
        (1, 1, 0, 0, 1, 255), (1, 0, 0, 0, 7, 255), (1, 1, 1, 0, 1, 255), (1, 2, 1, 1, 0, 255),
        (1, 3, 0, 3, 0, 255), (1, 2, 0, 1, 0, 255), (1, 0, 1, 0, 7, 255),
    ),
    (
        (0, 0, 0, 1, 255), (1, 1, 0, 0, 2, 255), (1, 2, 0, 1, 1, 255), (0, 0, 0, 7, 255),
        (1, 3, 0, 3, 7, 255), (1, 0, 0, 0, 6, 255), (0, 1, 0, 1, 255), (1, 1, 1, 0, 2, 255),
        (0, 1, 1, 0, 255), (1, 2, 1, 2, 0, 255), (1, 1, 1, 1, 1, 255), (1, 0, 1, 1, 7, 255),
        (0, 0, 0, 2, 255), (1, 1, 0, 0, 3, 255), (1, 2, 0, 1, 2, 255), (0, 0, 3, 0, 255),
        (1, 3, 0, 2, 0, 255), (0, 0, 3, 7, 255), (1, 3, 0, 2, 7, 255), (0, 0, 1, 0, 255),
        (1, 0, 0, 1, 7, 255),
    ),
    (
        (0, 0, 0, 6, 255), (1, 3, 0, 3, 6, 255), (1, 0, 0, 0, 5, 255), (1, 2, 0, 1, 6, 255),
        (0, 1, 0, 2, 255), (1, 2, 1, 1, 2, 255), (1, 1, 1, 0, 3, 195), (0, 0, 1, 1, 255),
        (1, 2, 0, 2, 1, 127), (0, 1, 2, 0, 255), (1, 0, 1, 2, 7, 255), (1, 1, 1, 2, 1, 254),
        (0, 0, 2, 0, 255),
    ),
    (
        (0, 0, 3, 6, 255), (1, 3, 0, 2, 6, 255), (0, 1, 1, 1, 255), (0, 1, 1, 7, 255), (1, 0, 1, 1, 6, 255),
        (0, 0, 0, 5, 255), (1, 2, 0, 1, 5, 255), (0, 1, 0, 7, 255), (1, 3, 1, 3, 7, 1), (1, 0, 1, 0, 6, 255),
        (0, 0, 1, 7, 255),
    ),
    (
        (0, 0, 0, 3, 255), (1, 2, 0, 1, 3, 255), (1, 1, 0, 0, 4, 225), (0, 1, 1, 2, 255),
        (1, 1, 1, 1, 3, 255), (0, 1, 2, 7, 255), (0, 0, 1, 2, 255), (1, 2, 0, 2, 2, 63), (0, 0, 2, 7, 255),
    ),
    (
        (0, 1, 3, 7, 1), (0, 0, 1, 5, 255), (1, 0, 0, 1, 4, 255), (1, 2, 0, 2, 5, 135), (0, 1, 1, 6, 255),
        (1, 0, 1, 1, 5, 255), (1, 2, 1, 2, 6, 255), (0, 0, 1, 3, 255), (1, 2, 0, 2, 3, 31), (0, 1, 2, 1, 127),
        (1, 1, 1, 2, 2, 126), (0, 0, 2, 1, 127),
    ),
    (
        (0, 1, 1, 3, 255), (1, 1, 1, 1, 4, 255), (1, 2, 1, 2, 3, 31), (0, 0, 1, 4, 255), (0, 1, 0, 3, 225),
        (1, 1, 1, 0, 4, 225), (0, 1, 0, 6, 255), (1, 0, 1, 0, 5, 124), (1, 3, 1, 3, 6, 3), (0, 0, 1, 6, 255),
    ),
    (
        (0, 0, 2, 6, 255), (0, 0, 2, 5, 135), (1, 0, 0, 2, 4, 135), (0, 0, 0, 4, 240), (0, 0, 2, 2, 63),
        (0, 0, 2, 3, 31), (0, 1, 1, 5, 255), (1, 2, 1, 2, 5, 7), (0, 1, 2, 2, 63), (0, 1, 2, 6, 255),
    ),
    (
        (0, 1, 0, 5, 248), (0, 1, 3, 6, 3), (0, 1, 1, 4, 255), (0, 1, 2, 3, 31), (1, 1, 1, 2, 4, 30),
    ),
    (
        (0, 1, 0, 4, 240), (0, 0, 2, 4, 15), (0, 1, 2, 5, 7), (0, 1, 2, 4, 15),
    ),
)
MESSAGES = tuple(item[1:] for tick in TICKS for item in tick if item[0] == 1)


def pick(index, numbers):
    value = jnp.int32(numbers[0])
    for at, number in enumerate(numbers[1:], 1):
        value = jnp.where(index == at, jnp.int32(number), value)
    return value


def kernel(
    q_ref, k_ref, v_ref, len_ref, w_ref, out_ref,
    qt, kv, acc, top, qpos, firsts, lasts, wts, att, far, near_r, near_l, mid_l, mid_r, in_l, in_r, mine,
    kv_send, kv_recv, w_local, w_send, w_recv, a_send, a_recv, x_send, x_recv,
):
    ctx, tp = lax.axis_index("ctx"), lax.axis_index("tp")
    y, z = ctx // NZ, lax.rem(ctx, NZ)
    x, core = tp // NK, lax.rem(tp, NK)
    z_next = (y * NZ + lax.rem(z + 1, NZ), tp)
    z_back = (y * NZ + lax.rem(z + NZ - 1, NZ), tp)
    y_next = (lax.rem(y + 1, NY) * NZ + z, tp)
    y_back = (lax.rem(y + NY - 1, NY) * NZ + z, tp)
    x_next = (ctx, lax.rem(x + 1, NX) * NK + core)
    x_back = (ctx, lax.rem(x + NX - 1, NX) * NK + core)
    other = (ctx, x * NK + 1 - core)
    links = (z_next, z_back, y_next, y_back)
    shift = ((0, 1), (0, -1), (-1, 0), (1, 0))

    barrier = pltpu.get_barrier_semaphore()
    for device in links + (x_next, x_back, other):
        pl.semaphore_signal(barrier, inc=1, device_id=device, device_id_type=MESH)

    values_t = v_ref[...].astype(jnp.float32).T.astype(jnp.bfloat16)
    for c in range(3):
        kv[0, z, c, 0:HEAD, :] = k_ref[c * HEAD:(c + 1) * HEAD, :]
        kv[0, z, c, HEAD:, :] = values_t[:, c * HEAD:(c + 1) * HEAD]

    def message(link, part, row, column):
        piece = pl.ds(0, 1) if part == 0 else pl.ds(1, 2)
        dy, dz = shift[link]
        held = (row + dy) % NY
        col = lax.rem(z + (column + dz) + 2 * NZ, NZ)
        return pltpu.make_async_remote_copy(
            src_ref=kv.at[held, col, piece],
            dst_ref=kv.at[row, col, piece],
            send_sem=kv_send.at[part, row, column],
            recv_sem=kv_recv.at[part, row, column],
            device_id=links[link],
            device_id_type=MESH,
        )

    def arrival(part, row, column):
        piece = pl.ds(0, 1) if part == 0 else pl.ds(1, 2)
        slot = kv.at[row, lax.rem(z + column, NZ), piece]
        return pltpu.make_async_remote_copy(
            src_ref=slot,
            dst_ref=slot,
            send_sem=kv_send.at[part, row, column],
            recv_sem=kv_recv.at[part, row, column],
            device_id=z_next,
            device_id_type=MESH,
        )

    def where(mask, run):
        if mask == (1 << NZ) - 1:
            run()
            return
        within = None
        for first in range(NZ):
            if mask >> first & 1 and not (first and mask >> (first - 1) & 1):
                last = first
                while mask >> (last + 1) & 1:
                    last += 1
                here = (z >= first) & (z <= last)
                within = here if within is None else within | here
        pl.when(within)(run)

    def act(item):
        if item[0] == 0:
            where(item[-1], lambda: arrival(*item[1:-1]).wait_recv())
        else:
            where(item[-1], lambda: message(*item[1:-1]).start())

    pl.semaphore_wait(barrier, 7)
    for item in TICKS[0]:
        act(item)

    def weight_columns(xx, half):
        return pl.ds(pl.multiple_of(xx * (2 * WIDE) + half * WIDE, HEAD), WIDE)

    def weight_keep(xx):
        return pltpu.make_async_copy(w_ref.at[:, weight_columns(xx, core)], wts.at[core, xx], w_local.at[xx])

    def weight_give(xx):
        return pltpu.make_async_remote_copy(
            src_ref=w_ref.at[:, weight_columns(xx, 1 - core)],
            dst_ref=wts.at[core, xx],
            send_sem=w_send.at[xx],
            recv_sem=w_recv.at[xx],
            device_id=other,
            device_id_type=MESH,
        )

    for xx in range(NX):
        weight_keep(xx).start()
        weight_give(xx).start()

    lane = lax.broadcasted_iota(jnp.int32, (8, HEAD), 1)
    sub = lax.broadcasted_iota(jnp.int32, (HEAD, ROWS), 0)
    first_l = jnp.where(lane == HEAD - 1, -(1 << 30), 0)
    last_l = jnp.zeros_like(lane)
    first_s, last_s = jnp.zeros_like(sub), jnp.zeros_like(sub)
    begin = jnp.int32(0)
    for d in range(24):
        end = begin + len_ref[d]
        first_l, last_l = jnp.where(lane == d, begin, first_l), jnp.where(lane == d, end, last_l)
        first_s, last_s = jnp.where(sub == d, begin, first_s), jnp.where(sub == d, end, last_s)
        begin = end
    firsts[...] = first_l
    lasts[...] = last_l
    own = ctx * ROWS + lax.broadcasted_iota(jnp.int32, (HEAD, ROWS), 1)
    apart = jnp.where((own >= first_s) & (own < last_s), 0.0, -BIG).astype(jnp.bfloat16)
    for h in range(GROUP):
        turned = q_ref[:, h * HEAD:(h + 1) * HEAD].astype(jnp.float32).T.astype(jnp.bfloat16)
        for t in range(TILES):
            span = slice(t * SPAN + h * TILE, t * SPAN + (h + 1) * TILE)
            rows = slice(t * TILE, (t + 1) * TILE)
            qt[0:HEAD, span] = turned[:, rows]
            qt[HEAD:, span] = apart[:, rows]
            qpos[:, span] = own[0:8, rows]
    top[...] = jnp.full_like(top, LOW)
    acc[...] = jnp.zeros_like(acc)

    def block(delta):
        row = (delta - z + NZ - 1) // NZ
        col = lax.rem(z - delta + 3 * NZ, NZ)
        held = kv[row, col]
        pos = (ctx - delta) * ROWS + lax.broadcasted_iota(jnp.int32, (ROWS, HEAD), 0)
        same = jnp.where((pos >= firsts[0:1, :]) & (pos < lasts[0:1, :]), 1.0, 0.0).astype(jnp.bfloat16)
        keys = jnp.concatenate([held[c, 0:HEAD] for c in range(3)], axis=0)
        vals = jnp.concatenate([held[c, HEAD:] for c in range(3)], axis=1)
        return jnp.concatenate([keys, same], axis=1), vals

    def attend(deltas, causal, base, steps):
        parts = [block(delta) for delta in deltas]
        keys = jnp.concatenate([part[0] for part in parts], axis=0)
        vals = jnp.concatenate([part[1] for part in parts], axis=1)
        count = keys.shape[0]
        vals = jnp.concatenate([vals, jnp.ones((16, count), jnp.bfloat16)], axis=0)

        def span_of(j):
            if isinstance(base, int):
                return slice(base + j * CHUNK, base + (j + 1) * CHUNK)
            return pl.ds(pl.multiple_of(base + j * CHUNK, CHUNK), CHUNK)

        def score(j):
            span = span_of(j)
            got = jnp.dot(keys, qt[:, span], preferred_element_type=jnp.float32)
            if causal:
                pos = (ctx - deltas[0]) * ROWS + lax.broadcasted_iota(jnp.int32, (count, CHUNK), 0)
                got = jnp.where(pos <= qpos[0:1, span], got, -BIG)
            return got

        def soften(j, got):
            span = span_of(j)
            old = top[0:1, span]
            new = jnp.maximum(old, jnp.max(got, axis=0, keepdims=True))
            top[0:1, span] = new
            return jnp.exp2((got - new) * SCALE).astype(jnp.bfloat16), jnp.exp2((old - new) * SCALE)

        def gather(j, weights, fade):
            span = span_of(j)
            acc[:, span] = acc[:, span] * fade + jnp.dot(vals, weights, preferred_element_type=jnp.float32)

        got, held = score(0), None
        for j in range(steps):
            ahead = score(j + 1) if j + 1 < steps else None
            soft = soften(j, got)
            if held is not None:
                gather(j - 1, *held)
            got, held = ahead, soft
        gather(steps - 1, *held)

    def step(i, carry):
        for at in range(1, len(ORDER)):
            @pl.when(i == at)
            def _(at=at):
                for item in TICKS[at]:
                    act(item)
        one = pick(i, [min(group) for group in ORDER])
        two = pick(i, [max(group) for group in ORDER])

        @pl.when((one == two) & (ctx >= one))
        def _():
            attend((one,), True, 0, COLS // CHUNK)

        @pl.when((one != two) & (ctx >= one))
        def _():
            attend((one, two), False, 0, COLS // CHUNK)

        return carry

    lax.fori_loop(0, len(ORDER), step, 0)

    for item in TICKS[len(ORDER)]:
        act(item)
    for xx in range(NX):
        weight_keep(xx).wait()
        weight_give(xx).wait()

    half = TILE // 2

    def swap(t):
        held = att.at[core, t]
        return pltpu.make_async_remote_copy(
            src_ref=held, dst_ref=held, send_sem=a_send.at[t], recv_sem=a_recv.at[t], device_id=other, device_id_type=MESH,
        )

    def along(t, at, src, dst, device):
        return pltpu.make_async_remote_copy(
            src_ref=src,
            dst_ref=dst,
            send_sem=x_send.at[t, at],
            recv_sem=x_recv.at[t, at],
            device_id=device,
            device_id_type=MESH,
        )

    lower, upper = pl.ds(0, half), pl.ds(half, half)

    def copies(t):
        return (
            along(t, 0, far.at[t, lower], mid_l.at[t], x_next),
            along(t, 1, far.at[t, upper], mid_r.at[t], x_back),
            along(t, 2, near_r.at[t, upper], in_l.at[t, upper], x_next),
            along(t, 3, near_l.at[t, lower], in_r.at[t, lower], x_back),
            along(t, 4, near_r.at[t, lower], in_l.at[t, lower], x_next),
            along(t, 5, near_l.at[t, upper], in_r.at[t, upper], x_back),
        )

    def pass_on(t):
        far_up, far_down, _, _, up, down = copies(t)
        far_up.wait_recv()
        near_r[t, 0:half] = (near_r[t, 0:half].astype(jnp.float32) + mid_l[t].astype(jnp.float32)).astype(jnp.bfloat16)
        up.start()
        far_down.wait_recv()
        near_l[t, half:] = (near_l[t, half:].astype(jnp.float32) + mid_r[t].astype(jnp.float32)).astype(jnp.bfloat16)
        down.start()

    def finish(t, carry):
        base = t * SPAN

        @pl.when(ctx >= min(LAST))
        def _():
            attend(LAST, False, base, SPAN // CHUNK)

        for h in range(GROUP):
            span = pl.ds(pl.multiple_of(base + h * TILE, TILE), TILE)
            rows = acc[0:HEAD, span] / acc[HEAD:HEAD + 1, span]
            att[core, t, :, h * HEAD:(h + 1) * HEAD] = rows.T.astype(jnp.bfloat16)
        swap(t).start()

        @pl.when(t > 0)
        def _():
            pass_on(t - 1)

        targets = [lax.rem(x + step, NX) for step in (2, 1, 3, 0)]
        sums = [jnp.dot(att[core, t], wts[core, xx], preferred_element_type=jnp.float32) for xx in targets]
        swap(t).wait()

        def whole(at):
            return sums[at] + jnp.dot(att[1 - core, t], wts[1 - core, targets[at]], preferred_element_type=jnp.float32)

        far_up, far_down, up, down, _, _ = copies(t)
        far[t] = whole(0).astype(jnp.bfloat16)
        far_up.start()
        far_down.start()
        near_r[t] = whole(1).astype(jnp.bfloat16)
        up.start()
        near_l[t] = whole(2).astype(jnp.bfloat16)
        down.start()
        mine[t] = whole(3)
        return carry

    lax.fori_loop(0, TILES, finish, 0)
    pass_on(TILES - 1)
    for t in range(TILES):
        for copy in copies(t)[2:]:
            copy.wait_recv()
        total = mine[t] + in_l[t].astype(jnp.float32) + in_r[t].astype(jnp.float32)
        out_ref[t * TILE:(t + 1) * TILE] = total.astype(jnp.bfloat16)
    for t in range(TILES):
        for copy in copies(t):
            copy.wait_send()
    for item in MESSAGES:
        where(item[-1], lambda item=item: message(*item[:-1]).wait_send())


def local(queries, keys, values, doc_lengths, out_weight):
    vmem = pl.BlockSpec(memory_space=pltpu.VMEM)
    bf16, f32 = jnp.bfloat16, jnp.float32
    dma = pltpu.SemaphoreType.DMA
    return pl.pallas_call(
        kernel,
        out_shape=jax.ShapeDtypeStruct((ROWS, WIDE), bf16),
        in_specs=[vmem, vmem, vmem, pl.BlockSpec(memory_space=pltpu.SMEM), pl.BlockSpec(memory_space=pl.ANY)],
        out_specs=vmem,
        scratch_shapes=[
            pltpu.VMEM((2 * HEAD, COLS), bf16),
            pltpu.VMEM((NY, NZ, 3, 2 * HEAD, HEAD), bf16),
            pltpu.VMEM((HEAD + 16, COLS), f32),
            pltpu.VMEM((8, COLS), f32),
            pltpu.VMEM((8, COLS), jnp.int32),
            pltpu.VMEM((8, HEAD), jnp.int32),
            pltpu.VMEM((8, HEAD), jnp.int32),
            pltpu.VMEM((NK, NX, GROUP * HEAD, WIDE), bf16),
            pltpu.VMEM((NK, TILES, TILE, GROUP * HEAD), bf16),
            pltpu.VMEM((TILES, TILE, WIDE), bf16),
            pltpu.VMEM((TILES, TILE, WIDE), bf16),
            pltpu.VMEM((TILES, TILE, WIDE), bf16),
            pltpu.VMEM((TILES, TILE // 2, WIDE), bf16),
            pltpu.VMEM((TILES, TILE // 2, WIDE), bf16),
            pltpu.VMEM((TILES, TILE, WIDE), bf16),
            pltpu.VMEM((TILES, TILE, WIDE), bf16),
            pltpu.VMEM((TILES, TILE, WIDE), f32),
            dma((2, NY, NZ)),
            dma((2, NY, NZ)),
            dma((NX,)),
            dma((NX,)),
            dma((NX,)),
            dma((TILES,)),
            dma((TILES,)),
            dma((TILES, 6)),
            dma((TILES, 6)),
        ],
        compiler_params=pltpu.CompilerParams(
            collective_id=0, has_side_effects=True, vmem_limit_bytes=60 << 20
        ),
    )(queries, keys, values, doc_lengths, out_weight)


def solution(mesh):
    in_specs = (P("ctx", "tp"), P("ctx", "tp"), P("ctx", "tp"), P(), P("tp", None))
    out_specs = P("ctx", "tp")
    return jax.shard_map(local, mesh=mesh, in_specs=in_specs, out_specs=out_specs, check_vma=False)
```

```python
import functools
import math

import jax
import jax.numpy as jnp
from jax import lax
from jax.experimental import pallas as pl
from jax.experimental.pallas import tpu as pltpu
from jax.sharding import PartitionSpec as P

MESH = pl.DeviceIdType.MESH
HEAD = 128
GROUP = 8
ROWS = 384
CHUNK = 512
NY, NZ, NX, NK = 4, 8, 4, 2
WIDE = 640
COLS = GROUP * ROWS
TILES = 3
TILE = ROWS // TILES
SPAN = GROUP * TILE
SCALE = math.log2(math.e) / math.sqrt(HEAD)
BIG = 262144.0
LOW = -1e30

SIZES = (2, 4, 4, 4, 4)
ORDER = (
    (7, 8, 1, 17, 18, 6, 5, 15, 2, 16, 9, 4, 3, 13, 14, 11, 10, 12),
    (1, 7, 8, 9, 18, 6, 5, 15, 2, 16, 17, 4, 3, 13, 14, 11, 10, 12),
    (1, 2, 7, 8, 9, 6, 5, 15, 10, 16, 17, 4, 3, 13, 14, 11, 18, 12),
    (1, 2, 7, 8, 9, 3, 6, 5, 15, 10, 16, 17, 4, 11, 13, 14, 18, 12),
    (1, 2, 7, 8, 9, 3, 6, 5, 15, 10, 16, 17, 12, 4, 11, 13, 14, 18),
    (1, 2, 7, 8, 9, 3, 6, 13, 15, 10, 16, 17, 12, 4, 11, 14, 18, 5),
    (1, 2, 7, 8, 9, 3, 14, 13, 6, 15, 10, 16, 17, 12, 4, 11, 18, 5),
    (1, 2, 15, 7, 8, 9, 3, 14, 13, 6, 10, 16, 17, 12, 4, 11, 18, 5),
)
TICKS = (
    (
        (1, 0, 0, 0, 7, 255), (1, 2, 0, 1, 0, 255), (1, 3, 0, 3, 0, 255), (1, 1, 1, 0, 1, 255),
        (1, 0, 1, 0, 7, 255), (1, 2, 1, 1, 0, 255), (1, 1, 0, 0, 1, 3),
    ),
    (
        (0, 0, 0, 7, 255), (1, 0, 0, 0, 6, 255), (1, 2, 0, 1, 7, 255), (1, 3, 0, 3, 7, 255),
        (0, 0, 1, 0, 255), (1, 1, 0, 1, 1, 255), (0, 0, 3, 0, 255), (1, 3, 0, 2, 0, 255), (0, 1, 0, 1, 255),
        (1, 2, 1, 1, 1, 255), (1, 1, 1, 0, 2, 129), (0, 1, 0, 7, 255), (1, 0, 1, 0, 6, 255),
        (1, 2, 1, 1, 7, 255), (1, 3, 1, 3, 7, 1), (0, 0, 0, 6, 255), (1, 0, 0, 0, 5, 255),
        (1, 3, 0, 3, 6, 255), (0, 0, 1, 1, 255), (1, 1, 0, 1, 2, 255), (0, 0, 2, 0, 255),
        (1, 1, 0, 2, 1, 254), (0, 1, 0, 6, 255), (1, 0, 1, 0, 5, 255), (1, 3, 1, 3, 6, 3), (0, 1, 1, 0, 255),
        (1, 2, 1, 2, 0, 255), (0, 1, 1, 1, 255), (1, 1, 1, 1, 2, 255), (1, 2, 1, 2, 1, 127),
        (0, 0, 0, 5, 255), (1, 0, 0, 0, 4, 120), (1, 3, 0, 3, 5, 135), (1, 2, 0, 1, 5, 255),
        (0, 0, 1, 2, 255), (1, 1, 0, 1, 3, 255), (0, 0, 1, 7, 255), (1, 0, 0, 1, 6, 255), (0, 0, 2, 1, 127),
        (1, 1, 0, 2, 2, 126), (0, 0, 3, 7, 255), (1, 3, 0, 2, 7, 255),
    ),
    (
        (0, 0, 0, 1, 129), (1, 1, 0, 0, 2, 129), (0, 0, 3, 6, 255), (1, 3, 0, 2, 6, 255), (0, 1, 1, 7, 255),
        (1, 0, 1, 1, 6, 255), (0, 1, 0, 5, 255), (1, 0, 1, 0, 4, 120), (1, 2, 1, 1, 5, 255),
        (0, 1, 1, 2, 255), (1, 1, 1, 1, 3, 255), (0, 1, 3, 6, 3), (0, 1, 3, 7, 1),
    ),
    (
        (0, 0, 0, 4, 240), (1, 0, 0, 0, 3, 112), (0, 0, 3, 5, 135), (1, 3, 0, 2, 5, 135), (0, 0, 2, 2, 63),
        (0, 0, 0, 2, 192), (0, 0, 1, 3, 255), (1, 1, 0, 1, 4, 255), (1, 2, 0, 2, 3, 31), (0, 1, 0, 2, 192),
        (0, 1, 1, 3, 255), (1, 2, 1, 2, 3, 31), (1, 1, 1, 1, 4, 255), (0, 1, 1, 6, 255), (1, 2, 1, 2, 6, 255),
        (0, 1, 2, 0, 255), (1, 0, 1, 2, 7, 255), (0, 1, 2, 1, 127), (1, 1, 1, 2, 2, 126), (0, 0, 1, 6, 255),
    ),
    (
        (0, 0, 2, 5, 135), (1, 0, 0, 2, 4, 135), (0, 1, 2, 3, 31), (1, 1, 1, 2, 4, 30), (0, 0, 1, 5, 255),
        (0, 1, 0, 4, 240), (1, 0, 1, 0, 3, 112), (0, 1, 1, 4, 255), (0, 1, 1, 5, 255), (1, 2, 1, 2, 5, 7),
        (0, 1, 2, 7, 255), (0, 0, 1, 4, 255), (0, 0, 2, 3, 31), (0, 0, 2, 7, 255),
    ),
    (
        (0, 1, 2, 4, 15), (0, 1, 2, 6, 255), (0, 1, 0, 3, 224), (0, 1, 2, 2, 63), (0, 1, 2, 5, 7),
        (0, 0, 0, 3, 224), (0, 0, 2, 4, 15), (0, 0, 2, 6, 255),
    ),
)
MESSAGES = tuple(item[1:] for tick in TICKS for item in tick if item[0] == 1)


def pick(index, numbers):
    value = jnp.int32(numbers[0])
    for at, number in enumerate(numbers[1:], 1):
        value = jnp.where(index == at, jnp.int32(number), value)
    return value


def kernel(
    q_ref, k_ref, v_ref, len_ref, w_ref, out_ref,
    q_own, qt, kv, acc, top, qpos, firsts, lasts, wts, att, far, near_r, near_l, mid_l, mid_r, in_l, in_r, mine,
    q_sem, kv_send, kv_recv, w_local, w_send, w_recv, a_send, a_recv, x_send, x_recv,
):
    ctx, tp = lax.axis_index("ctx"), lax.axis_index("tp")
    y, z = ctx // NZ, lax.rem(ctx, NZ)
    x, core = tp // NK, lax.rem(tp, NK)
    z_next = (y * NZ + lax.rem(z + 1, NZ), tp)
    z_back = (y * NZ + lax.rem(z + NZ - 1, NZ), tp)
    y_next = (lax.rem(y + 1, NY) * NZ + z, tp)
    y_back = (lax.rem(y + NY - 1, NY) * NZ + z, tp)
    x_next = (ctx, lax.rem(x + 1, NX) * NK + core)
    x_back = (ctx, lax.rem(x + NX - 1, NX) * NK + core)
    other = (ctx, x * NK + 1 - core)
    links = (z_next, z_back, y_next, y_back)
    shift = ((0, 1), (0, -1), (-1, 0), (1, 0))

    q_copy = pltpu.make_async_copy(q_ref, q_own, q_sem)
    q_copy.start()
    barrier = pltpu.get_barrier_semaphore()
    for device in links + (x_next, x_back, other):
        pl.semaphore_signal(barrier, inc=1, device_id=device, device_id_type=MESH)

    values_t = v_ref[...].astype(jnp.float32).T.astype(jnp.bfloat16)
    for c in range(3):
        kv[0, z, c, 0:HEAD, :] = k_ref[c * HEAD:(c + 1) * HEAD, :]
        kv[0, z, c, HEAD:, :] = values_t[:, c * HEAD:(c + 1) * HEAD]

    def message(link, part, row, column):
        piece = pl.ds(0, 1) if part == 0 else pl.ds(1, 2)
        dy, dz = shift[link]
        held = (row + dy) % NY
        col = lax.rem(z + (column + dz) + 2 * NZ, NZ)
        return pltpu.make_async_remote_copy(
            src_ref=kv.at[held, col, piece],
            dst_ref=kv.at[row, col, piece],
            send_sem=kv_send.at[part, row, column],
            recv_sem=kv_recv.at[part, row, column],
            device_id=links[link],
            device_id_type=MESH,
        )

    def arrival(part, row, column):
        piece = pl.ds(0, 1) if part == 0 else pl.ds(1, 2)
        slot = kv.at[row, lax.rem(z + column, NZ), piece]
        return pltpu.make_async_remote_copy(
            src_ref=slot,
            dst_ref=slot,
            send_sem=kv_send.at[part, row, column],
            recv_sem=kv_recv.at[part, row, column],
            device_id=z_next,
            device_id_type=MESH,
        )

    def where(mask, run):
        if mask == (1 << NZ) - 1:
            run()
            return
        within = None
        for first in range(NZ):
            if mask >> first & 1 and not (first and mask >> (first - 1) & 1):
                last = first
                while mask >> (last + 1) & 1:
                    last += 1
                here = (z >= first) & (z <= last)
                within = here if within is None else within | here
        pl.when(within)(run)

    def act(item):
        if item[0] == 0:
            where(item[-1], lambda: arrival(*item[1:-1]).wait_recv())
        else:
            where(item[-1], lambda: message(*item[1:-1]).start())

    pl.semaphore_wait(barrier, 7)
    for item in TICKS[0]:
        act(item)

    def weight_columns(xx, half):
        return pl.ds(pl.multiple_of(xx * (2 * WIDE) + half * WIDE, HEAD), WIDE)

    targets = [lax.rem(x + ahead, NX) for ahead in (2, 1, 3, 0)]

    def weight_keep(at):
        return pltpu.make_async_copy(
            w_ref.at[:, weight_columns(targets[at], core)], wts.at[core, :, pl.ds(at * WIDE, WIDE)], w_local.at[at]
        )

    def weight_give(at):
        return pltpu.make_async_remote_copy(
            src_ref=w_ref.at[:, weight_columns(targets[at], 1 - core)],
            dst_ref=wts.at[core, :, pl.ds(at * WIDE, WIDE)],
            send_sem=w_send.at[at],
            recv_sem=w_recv.at[at],
            device_id=other,
            device_id_type=MESH,
        )

    for xx in range(NX):
        weight_keep(xx).start()
        weight_give(xx).start()

    lane = lax.broadcasted_iota(jnp.int32, (8, HEAD), 1)
    sub = lax.broadcasted_iota(jnp.int32, (HEAD, ROWS), 0)
    first_l = jnp.where(lane == HEAD - 1, -(1 << 30), 0)
    last_l = jnp.zeros_like(lane)
    first_s, last_s = jnp.zeros_like(sub), jnp.zeros_like(sub)
    begin = jnp.int32(0)
    for d in range(24):
        end = begin + len_ref[d]
        first_l, last_l = jnp.where(lane == d, begin, first_l), jnp.where(lane == d, end, last_l)
        first_s, last_s = jnp.where(sub == d, begin, first_s), jnp.where(sub == d, end, last_s)
        begin = end
    firsts[...] = first_l
    lasts[...] = last_l
    own = ctx * ROWS + lax.broadcasted_iota(jnp.int32, (HEAD, ROWS), 1)
    apart = jnp.where((own >= first_s) & (own < last_s), 0.0, -BIG).astype(jnp.bfloat16)
    q_copy.wait()
    for h in range(GROUP):
        turned = q_own[:, h * HEAD:(h + 1) * HEAD].astype(jnp.float32).T.astype(jnp.bfloat16)
        for t in range(TILES):
            span = slice(t * SPAN + h * TILE, t * SPAN + (h + 1) * TILE)
            rows = slice(t * TILE, (t + 1) * TILE)
            qt[0:HEAD, span] = turned[:, rows]
            qt[HEAD:, span] = apart[:, rows]
            qpos[:, span] = own[0:8, rows]
    top[...] = jnp.full_like(top, LOW)
    acc[...] = jnp.zeros_like(acc)

    def block(delta):
        row = (delta - z + NZ - 1) // NZ
        col = lax.rem(z - delta + 3 * NZ, NZ)
        held = kv[row, col]
        pos = (ctx - delta) * ROWS + lax.broadcasted_iota(jnp.int32, (ROWS, HEAD), 0)
        same = jnp.where((pos >= firsts[0:1, :]) & (pos < lasts[0:1, :]), 1.0, 0.0).astype(jnp.bfloat16)
        keys = jnp.concatenate([held[c, 0:HEAD] for c in range(3)], axis=0)
        vals = jnp.concatenate([held[c, HEAD:] for c in range(3)], axis=1)
        return jnp.concatenate([keys, same], axis=1), vals

    def attend(deltas, causal, base, steps):
        parts = [block(delta) for delta in deltas]
        keys = jnp.concatenate([part[0] for part in parts], axis=0)
        vals = jnp.concatenate([part[1] for part in parts], axis=1)
        count = keys.shape[0]
        vals = jnp.concatenate([vals, jnp.ones((16, count), jnp.bfloat16)], axis=0)

        def span_of(j):
            if isinstance(base, int):
                return slice(base + j * CHUNK, base + (j + 1) * CHUNK)
            return pl.ds(pl.multiple_of(base + j * CHUNK, CHUNK), CHUNK)

        def score(j):
            span = span_of(j)
            got = jnp.dot(keys, qt[:, span], preferred_element_type=jnp.float32)
            if causal:
                pos = (ctx - deltas[0]) * ROWS + lax.broadcasted_iota(jnp.int32, (count, CHUNK), 0)
                got = jnp.where(pos <= qpos[0:1, span], got, -BIG)
            return got

        def soften(j, got):
            span = span_of(j)
            old = top[0:1, span]
            new = jnp.maximum(old, jnp.max(got, axis=0, keepdims=True))
            top[0:1, span] = new
            return jnp.exp2((got - new) * SCALE).astype(jnp.bfloat16), jnp.exp2((old - new) * SCALE)

        def gather(j, weights, fade):
            span = span_of(j)
            acc[:, span] = acc[:, span] * fade + jnp.dot(vals, weights, preferred_element_type=jnp.float32)

        got, held = score(0), None
        for j in range(steps):
            ahead = score(j + 1) if j + 1 < steps else None
            soft = soften(j, got)
            if held is not None:
                gather(j - 1, *held)
            got, held = ahead, soft
        gather(steps - 1, *held)

    order = [pick(z, [row[at] for row in ORDER]) for at in range(len(ORDER[0]))]
    groups, at = [[jnp.int32(0)]], 0
    for size in SIZES:
        groups.append(order[at:at + size])
        at += size
    last = groups.pop()
    sizes = [len(group) for group in groups]

    def least(deltas):
        return functools.reduce(jnp.minimum, deltas)

    def step(i, carry):
        for at in range(1, len(groups)):
            @pl.when(i == at)
            def _(at=at):
                for item in TICKS[at]:
                    act(item)

        for size in sorted(set(sizes)):
            deltas = []
            for slot in range(size):
                value = groups[0][0]
                for at, group in enumerate(groups):
                    if len(group) == size:
                        value = jnp.where(i == at, group[slot], value)
                deltas.append(value)
            now = functools.reduce(jnp.logical_or, [i == at for at in range(len(groups)) if sizes[at] == size])

            @pl.when(now & (ctx >= least(deltas)))
            def _(deltas=tuple(deltas), size=size):
                attend(deltas, size == 1, 0, COLS // CHUNK)

        return carry

    lax.fori_loop(0, len(groups), step, 0)

    for item in TICKS[len(groups)]:
        act(item)
    for xx in range(NX):
        weight_keep(xx).wait()
        weight_give(xx).wait()

    half = TILE // 2

    def swap(t):
        held = att.at[core, t]
        return pltpu.make_async_remote_copy(
            src_ref=held, dst_ref=held, send_sem=a_send.at[t], recv_sem=a_recv.at[t], device_id=other, device_id_type=MESH,
        )

    def along(t, at, src, dst, device):
        return pltpu.make_async_remote_copy(
            src_ref=src,
            dst_ref=dst,
            send_sem=x_send.at[t, at],
            recv_sem=x_recv.at[t, at],
            device_id=device,
            device_id_type=MESH,
        )

    lower, upper = pl.ds(0, half), pl.ds(half, half)

    def copies(t):
        return (
            along(t, 0, far.at[t, lower], mid_l.at[t], x_next),
            along(t, 1, far.at[t, upper], mid_r.at[t], x_back),
            along(t, 2, near_r.at[t, upper], in_l.at[t, upper], x_next),
            along(t, 3, near_l.at[t, lower], in_r.at[t, lower], x_back),
            along(t, 4, near_r.at[t, lower], in_l.at[t, lower], x_next),
            along(t, 5, near_l.at[t, upper], in_r.at[t, upper], x_back),
        )

    def pass_on(t):
        far_up, far_down, _, _, up, down = copies(t)
        far_up.wait_recv()
        near_r[t, 0:half] = (near_r[t, 0:half].astype(jnp.float32) + mid_l[t].astype(jnp.float32)).astype(jnp.bfloat16)
        up.start()
        far_down.wait_recv()
        near_l[t, half:] = (near_l[t, half:].astype(jnp.float32) + mid_r[t].astype(jnp.float32)).astype(jnp.bfloat16)
        down.start()

    def finish(t, carry):
        base = t * SPAN

        @pl.when(ctx >= least(last))
        def _():
            attend(tuple(last), False, base, SPAN // CHUNK)

        for h in range(GROUP):
            span = pl.ds(pl.multiple_of(base + h * TILE, TILE), TILE)
            rows = acc[0:HEAD, span] * (1.0 / acc[HEAD:HEAD + 1, span])
            att[core, t, :, h * HEAD:(h + 1) * HEAD] = rows.T.astype(jnp.bfloat16)
        swap(t).start()

        @pl.when(t > 0)
        def _():
            pass_on(t - 1)

        def term(of, at):
            return jnp.dot(att[of, t], wts[of, :, 2 * at * WIDE:2 * (at + 1) * WIDE], preferred_element_type=jnp.float32)

        far_up, far_down, up, down, _, _ = copies(t)
        total = term(core, 0)
        swap(t).wait()
        total += term(1 - core, 0)
        far[t] = total[:, 0:WIDE].astype(jnp.bfloat16)
        far_up.start()
        far_down.start()
        near_r[t] = total[:, WIDE:].astype(jnp.bfloat16)
        up.start()
        total = term(core, 1) + term(1 - core, 1)
        near_l[t] = total[:, 0:WIDE].astype(jnp.bfloat16)
        down.start()
        mine[t] = total[:, WIDE:]
        return carry

    lax.fori_loop(0, TILES, finish, 0)
    pass_on(TILES - 1)
    for t in range(TILES):
        for copy in copies(t)[2:]:
            copy.wait_recv()
        total = mine[t] + in_l[t].astype(jnp.float32) + in_r[t].astype(jnp.float32)
        out_ref[t * TILE:(t + 1) * TILE] = total.astype(jnp.bfloat16)
    for t in range(TILES):
        for copy in copies(t):
            copy.wait_send()
    for item in MESSAGES:
        where(item[-1], lambda item=item: message(*item[:-1]).wait_send())


def local(queries, keys, values, doc_lengths, out_weight):
    vmem = pl.BlockSpec(memory_space=pltpu.VMEM)
    bf16, f32 = jnp.bfloat16, jnp.float32
    dma = pltpu.SemaphoreType.DMA
    return pl.pallas_call(
        kernel,
        out_shape=jax.ShapeDtypeStruct((ROWS, WIDE), bf16),
        in_specs=[pl.BlockSpec(memory_space=pl.ANY), vmem, vmem, pl.BlockSpec(memory_space=pltpu.SMEM), pl.BlockSpec(memory_space=pl.ANY)],
        out_specs=vmem,
        scratch_shapes=[
            pltpu.VMEM((ROWS, GROUP * HEAD), bf16),
            pltpu.VMEM((2 * HEAD, COLS), bf16),
            pltpu.VMEM((NY, NZ, 3, 2 * HEAD, HEAD), bf16),
            pltpu.VMEM((HEAD + 16, COLS), f32),
            pltpu.VMEM((8, COLS), f32),
            pltpu.VMEM((8, COLS), jnp.int32),
            pltpu.VMEM((8, HEAD), jnp.int32),
            pltpu.VMEM((8, HEAD), jnp.int32),
            pltpu.VMEM((NK, GROUP * HEAD, NX * WIDE), bf16),
            pltpu.VMEM((NK, TILES, TILE, GROUP * HEAD), bf16),
            pltpu.VMEM((TILES, TILE, WIDE), bf16),
            pltpu.VMEM((TILES, TILE, WIDE), bf16),
            pltpu.VMEM((TILES, TILE, WIDE), bf16),
            pltpu.VMEM((TILES, TILE // 2, WIDE), bf16),
            pltpu.VMEM((TILES, TILE // 2, WIDE), bf16),
            pltpu.VMEM((TILES, TILE, WIDE), bf16),
            pltpu.VMEM((TILES, TILE, WIDE), bf16),
            pltpu.VMEM((TILES, TILE, WIDE), f32),
            dma,
            dma((2, NY, NZ)),
            dma((2, NY, NZ)),
            dma((NX,)),
            dma((NX,)),
            dma((NX,)),
            dma((TILES,)),
            dma((TILES,)),
            dma((TILES, 6)),
            dma((TILES, 6)),
        ],
        compiler_params=pltpu.CompilerParams(
            collective_id=0, has_side_effects=True, vmem_limit_bytes=60 << 20
        ),
    )(queries, keys, values, doc_lengths, out_weight)


def solution(mesh):
    in_specs = (P("ctx", "tp"), P("ctx", "tp"), P("ctx", "tp"), P(), P("tp", None))
    out_specs = P("ctx", "tp")
    return jax.shard_map(local, mesh=mesh, in_specs=in_specs, out_specs=out_specs, check_vma=False)
```

```python
import functools
import math

import jax
import jax.numpy as jnp
from jax import lax
from jax.experimental import pallas as pl
from jax.experimental.pallas import tpu as pltpu
from jax.sharding import PartitionSpec as P

MESH = pl.DeviceIdType.MESH
HEAD = 128
GROUP = 8
ROWS = 384
CHUNK = 512
NY, NZ, NX, NK = 4, 8, 4, 2
WIDE = 640
COLS = GROUP * ROWS
TILES = 3
TILE = ROWS // TILES
SPAN = GROUP * TILE
SCALE = math.log2(math.e) / math.sqrt(HEAD)
BIG = 262144.0
LOW = -1e30

SIZES = (2, 4, 4, 4, 4)
ORDER = (
    (7, 8, 1, 17, 18, 6, 5, 15, 2, 16, 9, 4, 3, 13, 14, 11, 10, 12),
    (1, 7, 8, 9, 18, 6, 5, 15, 2, 16, 17, 4, 3, 13, 14, 11, 10, 12),
    (1, 2, 7, 8, 9, 6, 5, 15, 10, 16, 17, 4, 3, 13, 14, 11, 18, 12),
    (1, 2, 7, 8, 9, 3, 6, 5, 15, 10, 16, 17, 4, 11, 13, 14, 18, 12),
    (1, 2, 7, 8, 9, 3, 6, 5, 15, 10, 16, 17, 12, 4, 11, 13, 14, 18),
    (1, 2, 7, 8, 9, 3, 6, 13, 15, 10, 16, 17, 12, 4, 11, 14, 18, 5),
    (1, 2, 7, 8, 9, 3, 14, 13, 6, 15, 10, 16, 17, 12, 4, 11, 18, 5),
    (1, 2, 15, 7, 8, 9, 3, 14, 13, 6, 10, 16, 17, 12, 4, 11, 18, 5),
)
TICKS = (
    (
        (1, 0, 0, 0, 7, 255), (1, 2, 0, 1, 0, 255), (1, 3, 0, 3, 0, 255), (1, 1, 1, 0, 1, 255),
        (1, 0, 1, 0, 7, 255), (1, 2, 1, 1, 0, 255), (1, 1, 0, 0, 1, 3),
    ),
    (
        (0, 0, 0, 7, 255), (1, 0, 0, 0, 6, 255), (1, 2, 0, 1, 7, 255), (1, 3, 0, 3, 7, 255),
        (0, 0, 1, 0, 255), (1, 1, 0, 1, 1, 255), (0, 0, 3, 0, 255), (1, 3, 0, 2, 0, 255), (0, 1, 0, 1, 255),
        (1, 2, 1, 1, 1, 255), (1, 1, 1, 0, 2, 129), (0, 1, 0, 7, 255), (1, 0, 1, 0, 6, 255),
        (1, 2, 1, 1, 7, 255), (1, 3, 1, 3, 7, 1), (0, 0, 0, 6, 255), (1, 0, 0, 0, 5, 255),
        (1, 3, 0, 3, 6, 255), (0, 0, 1, 1, 255), (1, 1, 0, 1, 2, 255), (0, 0, 2, 0, 255),
        (1, 1, 0, 2, 1, 254), (0, 1, 0, 6, 255), (1, 0, 1, 0, 5, 255), (1, 3, 1, 3, 6, 3), (0, 1, 1, 0, 255),
        (1, 2, 1, 2, 0, 255), (0, 1, 1, 1, 255), (1, 1, 1, 1, 2, 255), (1, 2, 1, 2, 1, 127),
        (0, 0, 0, 5, 255), (1, 0, 0, 0, 4, 120), (1, 3, 0, 3, 5, 135), (1, 2, 0, 1, 5, 255),
        (0, 0, 1, 2, 255), (1, 1, 0, 1, 3, 255), (0, 0, 1, 7, 255), (1, 0, 0, 1, 6, 255), (0, 0, 2, 1, 127),
        (1, 1, 0, 2, 2, 126), (0, 0, 3, 7, 255), (1, 3, 0, 2, 7, 255),
    ),
    (
        (0, 0, 0, 1, 129), (1, 1, 0, 0, 2, 129), (0, 0, 3, 6, 255), (1, 3, 0, 2, 6, 255), (0, 1, 1, 7, 255),
        (1, 0, 1, 1, 6, 255), (0, 1, 0, 5, 255), (1, 0, 1, 0, 4, 120), (1, 2, 1, 1, 5, 255),
        (0, 1, 1, 2, 255), (1, 1, 1, 1, 3, 255), (0, 1, 3, 6, 3), (0, 1, 3, 7, 1),
    ),
    (
        (0, 0, 0, 4, 240), (1, 0, 0, 0, 3, 112), (0, 0, 3, 5, 135), (1, 3, 0, 2, 5, 135), (0, 0, 2, 2, 63),
        (0, 0, 0, 2, 192), (0, 0, 1, 3, 255), (1, 1, 0, 1, 4, 255), (1, 2, 0, 2, 3, 31), (0, 1, 0, 2, 192),
        (0, 1, 1, 3, 255), (1, 2, 1, 2, 3, 31), (1, 1, 1, 1, 4, 255), (0, 1, 1, 6, 255), (1, 2, 1, 2, 6, 255),
        (0, 1, 2, 0, 255), (1, 0, 1, 2, 7, 255), (0, 1, 2, 1, 127), (1, 1, 1, 2, 2, 126), (0, 0, 1, 6, 255),
    ),
    (
        (0, 0, 2, 5, 135), (1, 0, 0, 2, 4, 135), (0, 1, 2, 3, 31), (1, 1, 1, 2, 4, 30), (0, 0, 1, 5, 255),
        (0, 1, 0, 4, 240), (1, 0, 1, 0, 3, 112), (0, 1, 1, 4, 255), (0, 1, 1, 5, 255), (1, 2, 1, 2, 5, 7),
        (0, 1, 2, 7, 255), (0, 0, 1, 4, 255), (0, 0, 2, 3, 31), (0, 0, 2, 7, 255),
    ),
    (
        (0, 1, 2, 4, 15), (0, 1, 2, 6, 255), (0, 1, 0, 3, 224), (0, 1, 2, 2, 63), (0, 1, 2, 5, 7),
        (0, 0, 0, 3, 224), (0, 0, 2, 4, 15), (0, 0, 2, 6, 255),
    ),
)
MESSAGES = tuple(item[1:] for tick in TICKS for item in tick if item[0] == 1)


def pick(index, numbers):
    value = jnp.int32(numbers[0])
    for at, number in enumerate(numbers[1:], 1):
        value = jnp.where(index == at, jnp.int32(number), value)
    return value


def kernel(
    q_ref, k_ref, v_ref, len_ref, w_ref, out_ref,
    q_own, qt, kv, acc, top, qpos, firsts, lasts, wts, att, far, near_r, near_l, mid_l, mid_r, in_l, in_r, mine,
    q_sem, kv_send, kv_recv, w_local, w_send, w_recv, a_send, a_recv, x_send, x_recv,
):
    ctx, tp = lax.axis_index("ctx"), lax.axis_index("tp")
    y, z = ctx // NZ, lax.rem(ctx, NZ)
    x, core = tp // NK, lax.rem(tp, NK)
    z_next = (y * NZ + lax.rem(z + 1, NZ), tp)
    z_back = (y * NZ + lax.rem(z + NZ - 1, NZ), tp)
    y_next = (lax.rem(y + 1, NY) * NZ + z, tp)
    y_back = (lax.rem(y + NY - 1, NY) * NZ + z, tp)
    x_next = (ctx, lax.rem(x + 1, NX) * NK + core)
    x_back = (ctx, lax.rem(x + NX - 1, NX) * NK + core)
    other = (ctx, x * NK + 1 - core)
    links = (z_next, z_back, y_next, y_back)
    shift = ((0, 1), (0, -1), (-1, 0), (1, 0))

    q_copy = pltpu.make_async_copy(q_ref, q_own, q_sem)
    q_copy.start()
    barrier = pltpu.get_barrier_semaphore()
    for device in links + (x_next, x_back, other):
        pl.semaphore_signal(barrier, inc=1, device_id=device, device_id_type=MESH)

    values_t = v_ref[...].astype(jnp.float32).T.astype(jnp.bfloat16)
    for c in range(3):
        kv[0, z, c, 0:HEAD, :] = k_ref[c * HEAD:(c + 1) * HEAD, :]
        kv[0, z, c, HEAD:, :] = values_t[:, c * HEAD:(c + 1) * HEAD]

    def message(link, part, row, column):
        piece = pl.ds(0, 1) if part == 0 else pl.ds(1, 2)
        dy, dz = shift[link]
        held = (row + dy) % NY
        col = lax.rem(z + (column + dz) + 2 * NZ, NZ)
        return pltpu.make_async_remote_copy(
            src_ref=kv.at[held, col, piece],
            dst_ref=kv.at[row, col, piece],
            send_sem=kv_send.at[part, row, column],
            recv_sem=kv_recv.at[part, row, column],
            device_id=links[link],
            device_id_type=MESH,
        )

    def arrival(part, row, column):
        piece = pl.ds(0, 1) if part == 0 else pl.ds(1, 2)
        slot = kv.at[row, lax.rem(z + column, NZ), piece]
        return pltpu.make_async_remote_copy(
            src_ref=slot,
            dst_ref=slot,
            send_sem=kv_send.at[part, row, column],
            recv_sem=kv_recv.at[part, row, column],
            device_id=z_next,
            device_id_type=MESH,
        )

    def where(mask, run):
        if mask == (1 << NZ) - 1:
            run()
            return
        within = None
        for first in range(NZ):
            if mask >> first & 1 and not (first and mask >> (first - 1) & 1):
                last = first
                while mask >> (last + 1) & 1:
                    last += 1
                here = (z >= first) & (z <= last)
                within = here if within is None else within | here
        pl.when(within)(run)

    def act(item):
        if item[0] == 0:
            where(item[-1], lambda: arrival(*item[1:-1]).wait_recv())
        else:
            where(item[-1], lambda: message(*item[1:-1]).start())

    pl.semaphore_wait(barrier, 7)
    for item in TICKS[0]:
        act(item)

    def weight_columns(xx, half):
        return pl.ds(pl.multiple_of(xx * (2 * WIDE) + half * WIDE, HEAD), WIDE)

    targets = [lax.rem(x + ahead, NX) for ahead in (2, 1, 3, 0)]

    def weight_keep(at):
        return pltpu.make_async_copy(
            w_ref.at[:, weight_columns(targets[at], core)], wts.at[core, :, pl.ds(at * WIDE, WIDE)], w_local.at[at]
        )

    def weight_give(at):
        return pltpu.make_async_remote_copy(
            src_ref=w_ref.at[:, weight_columns(targets[at], 1 - core)],
            dst_ref=wts.at[core, :, pl.ds(at * WIDE, WIDE)],
            send_sem=w_send.at[at],
            recv_sem=w_recv.at[at],
            device_id=other,
            device_id_type=MESH,
        )

    for xx in range(NX):
        weight_keep(xx).start()
        weight_give(xx).start()

    lane = lax.broadcasted_iota(jnp.int32, (8, HEAD), 1)
    sub = lax.broadcasted_iota(jnp.int32, (HEAD, ROWS), 0)
    first_l = jnp.where(lane == HEAD - 1, -(1 << 30), 0)
    last_l = jnp.zeros_like(lane)
    first_s, last_s = jnp.zeros_like(sub), jnp.zeros_like(sub)
    begin = jnp.int32(0)
    for d in range(24):
        end = begin + len_ref[d]
        first_l, last_l = jnp.where(lane == d, begin, first_l), jnp.where(lane == d, end, last_l)
        first_s, last_s = jnp.where(sub == d, begin, first_s), jnp.where(sub == d, end, last_s)
        begin = end
    firsts[...] = first_l
    lasts[...] = last_l
    own = ctx * ROWS + lax.broadcasted_iota(jnp.int32, (HEAD, ROWS), 1)
    apart = jnp.where((own >= first_s) & (own < last_s), 0.0, -BIG).astype(jnp.bfloat16)
    q_copy.wait()
    for h in range(GROUP):
        turned = q_own[:, h * HEAD:(h + 1) * HEAD].astype(jnp.float32).T.astype(jnp.bfloat16)
        for t in range(TILES):
            span = slice(t * SPAN + h * TILE, t * SPAN + (h + 1) * TILE)
            rows = slice(t * TILE, (t + 1) * TILE)
            qt[0:HEAD, span] = turned[:, rows]
            qt[HEAD:, span] = apart[:, rows]
            qpos[:, span] = own[0:8, rows]
    top[...] = jnp.full_like(top, LOW)
    acc[...] = jnp.zeros_like(acc)

    def block(delta):
        row = (delta - z + NZ - 1) // NZ
        col = lax.rem(z - delta + 3 * NZ, NZ)
        held = kv[row, col]
        pos = (ctx - delta) * ROWS + lax.broadcasted_iota(jnp.int32, (ROWS, HEAD), 0)
        same = jnp.where((pos >= firsts[0:1, :]) & (pos < lasts[0:1, :]), 1.0, 0.0).astype(jnp.bfloat16)
        keys = jnp.concatenate([held[c, 0:HEAD] for c in range(3)], axis=0)
        vals = jnp.concatenate([held[c, HEAD:] for c in range(3)], axis=1)
        return jnp.concatenate([keys, same], axis=1), vals

    def attend(deltas, causal, base, steps):
        parts = [block(delta) for delta in deltas]
        keys = jnp.concatenate([part[0] for part in parts], axis=0)
        vals = jnp.concatenate([part[1] for part in parts], axis=1)
        count = keys.shape[0]
        vals = jnp.concatenate([vals, jnp.ones((16, count), jnp.bfloat16)], axis=0)

        def span_of(j):
            if isinstance(base, int):
                return slice(base + j * CHUNK, base + (j + 1) * CHUNK)
            return pl.ds(pl.multiple_of(base + j * CHUNK, CHUNK), CHUNK)

        def score(j):
            span = span_of(j)
            got = jnp.dot(keys, qt[:, span], preferred_element_type=jnp.float32)
            if causal:
                pos = (ctx - deltas[0]) * ROWS + lax.broadcasted_iota(jnp.int32, (count, CHUNK), 0)
                got = jnp.where(pos <= qpos[0:1, span], got, -BIG)
            return got

        def soften(j, got):
            span = span_of(j)
            old = top[0:1, span]
            new = jnp.maximum(old, jnp.max(got, axis=0, keepdims=True))
            top[0:1, span] = new
            return jnp.exp2((got - new) * SCALE).astype(jnp.bfloat16), jnp.exp2((old - new) * SCALE)

        def gather(j, weights, fade):
            span = span_of(j)
            acc[:, span] = acc[:, span] * fade + jnp.dot(vals, weights, preferred_element_type=jnp.float32)

        got, held = score(0), None
        for j in range(steps):
            ahead = score(j + 1) if j + 1 < steps else None
            soft = soften(j, got)
            if held is not None:
                gather(j - 1, *held)
            got, held = ahead, soft
        gather(steps - 1, *held)

    order = [pick(z, [row[at] for row in ORDER]) for at in range(len(ORDER[0]))]
    groups, at = [[jnp.int32(0)]], 0
    for size in SIZES:
        groups.append(order[at:at + size])
        at += size
    last = groups.pop()
    sizes = [len(group) for group in groups]

    def least(deltas):
        return functools.reduce(jnp.minimum, deltas)

    def step(i, carry):
        for at in range(1, len(groups)):
            @pl.when(i == at)
            def _(at=at):
                for item in TICKS[at]:
                    act(item)

        for size in sorted(set(sizes)):
            deltas = []
            for slot in range(size):
                value = groups[0][0]
                for at, group in enumerate(groups):
                    if len(group) == size:
                        value = jnp.where(i == at, group[slot], value)
                deltas.append(value)
            now = functools.reduce(jnp.logical_or, [i == at for at in range(len(groups)) if sizes[at] == size])

            @pl.when(now & (ctx >= least(deltas)))
            def _(deltas=tuple(deltas), size=size):
                attend(deltas, size == 1, 0, COLS // CHUNK)

        return carry

    lax.fori_loop(0, len(groups), step, 0)

    for item in TICKS[len(groups)]:
        act(item)
    for xx in range(NX):
        weight_keep(xx).wait()
        weight_give(xx).wait()

    half = TILE // 2

    def swap(t):
        held = att.at[core, t]
        return pltpu.make_async_remote_copy(
            src_ref=held, dst_ref=held, send_sem=a_send.at[t], recv_sem=a_recv.at[t], device_id=other, device_id_type=MESH,
        )

    def along(t, at, src, dst, device):
        return pltpu.make_async_remote_copy(
            src_ref=src,
            dst_ref=dst,
            send_sem=x_send.at[t, at],
            recv_sem=x_recv.at[t, at],
            device_id=device,
            device_id_type=MESH,
        )

    lower, upper = pl.ds(0, half), pl.ds(half, half)

    def copies(t):
        return (
            along(t, 0, far.at[t, lower], mid_l.at[t], x_next),
            along(t, 1, far.at[t, upper], mid_r.at[t], x_back),
            along(t, 2, near_r.at[t, upper], in_l.at[t, upper], x_next),
            along(t, 3, near_l.at[t, lower], in_r.at[t, lower], x_back),
            along(t, 4, near_r.at[t, lower], in_l.at[t, lower], x_next),
            along(t, 5, near_l.at[t, upper], in_r.at[t, upper], x_back),
        )

    def pass_on(t):
        far_up, far_down, _, _, up, down = copies(t)
        far_up.wait_recv()
        near_r[t, 0:half] = (near_r[t, 0:half].astype(jnp.float32) + mid_l[t].astype(jnp.float32)).astype(jnp.bfloat16)
        up.start()
        far_down.wait_recv()
        near_l[t, half:] = (near_l[t, half:].astype(jnp.float32) + mid_r[t].astype(jnp.float32)).astype(jnp.bfloat16)
        down.start()

    def finish(t, carry):
        base = t * SPAN

        @pl.when(ctx >= least(last))
        def _():
            attend(tuple(last), False, base, SPAN // CHUNK)

        for h in range(GROUP):
            span = pl.ds(pl.multiple_of(base + h * TILE, TILE), TILE)
            rows = acc[0:HEAD, span] * (1.0 / acc[HEAD:HEAD + 1, span])
            att[core, t, :, h * HEAD:(h + 1) * HEAD] = rows.T.astype(jnp.bfloat16)
        swap(t).start()

        @pl.when(t > 0)
        def _():
            pass_on(t - 1)

        def term(of, at):
            return jnp.dot(att[of, t], wts[of, :, 2 * at * WIDE:2 * (at + 1) * WIDE], preferred_element_type=jnp.float32)

        far_up, far_down, up, down, _, _ = copies(t)
        total = term(core, 0)
        swap(t).wait()
        total += term(1 - core, 0)
        far[t] = total[:, 0:WIDE].astype(jnp.bfloat16)
        far_up.start()
        far_down.start()
        near_r[t] = total[:, WIDE:].astype(jnp.bfloat16)
        total = term(core, 1) + term(1 - core, 1)
        near_l[t] = total[:, 0:WIDE].astype(jnp.bfloat16)
        up.start()
        down.start()
        mine[t] = total[:, WIDE:]
        return carry

    lax.fori_loop(0, TILES, finish, 0)

    def add_up(t):
        for copy in copies(t)[2:]:
            copy.wait_recv()
        total = mine[t] + in_l[t].astype(jnp.float32) + in_r[t].astype(jnp.float32)
        out_ref[t * TILE:(t + 1) * TILE] = total.astype(jnp.bfloat16)

    for t in range(TILES - 2):
        add_up(t)
    pass_on(TILES - 1)
    for t in range(TILES - 2, TILES):
        add_up(t)
    for t in range(TILES):
        for copy in copies(t):
            copy.wait_send()
    for item in MESSAGES:
        where(item[-1], lambda item=item: message(*item[:-1]).wait_send())


def local(queries, keys, values, doc_lengths, out_weight):
    vmem = pl.BlockSpec(memory_space=pltpu.VMEM)
    bf16, f32 = jnp.bfloat16, jnp.float32
    dma = pltpu.SemaphoreType.DMA
    return pl.pallas_call(
        kernel,
        out_shape=jax.ShapeDtypeStruct((ROWS, WIDE), bf16),
        in_specs=[pl.BlockSpec(memory_space=pl.ANY), vmem, vmem, pl.BlockSpec(memory_space=pltpu.SMEM), pl.BlockSpec(memory_space=pl.ANY)],
        out_specs=vmem,
        scratch_shapes=[
            pltpu.VMEM((ROWS, GROUP * HEAD), bf16),
            pltpu.VMEM((2 * HEAD, COLS), bf16),
            pltpu.VMEM((NY, NZ, 3, 2 * HEAD, HEAD), bf16),
            pltpu.VMEM((HEAD + 16, COLS), f32),
            pltpu.VMEM((8, COLS), f32),
            pltpu.VMEM((8, COLS), jnp.int32),
            pltpu.VMEM((8, HEAD), jnp.int32),
            pltpu.VMEM((8, HEAD), jnp.int32),
            pltpu.VMEM((NK, GROUP * HEAD, NX * WIDE), bf16),
            pltpu.VMEM((NK, TILES, TILE, GROUP * HEAD), bf16),
            pltpu.VMEM((TILES, TILE, WIDE), bf16),
            pltpu.VMEM((TILES, TILE, WIDE), bf16),
            pltpu.VMEM((TILES, TILE, WIDE), bf16),
            pltpu.VMEM((TILES, TILE // 2, WIDE), bf16),
            pltpu.VMEM((TILES, TILE // 2, WIDE), bf16),
            pltpu.VMEM((TILES, TILE, WIDE), bf16),
            pltpu.VMEM((TILES, TILE, WIDE), bf16),
            pltpu.VMEM((TILES, TILE, WIDE), f32),
            dma,
            dma((2, NY, NZ)),
            dma((2, NY, NZ)),
            dma((NX,)),
            dma((NX,)),
            dma((NX,)),
            dma((TILES,)),
            dma((TILES,)),
            dma((TILES, 6)),
            dma((TILES, 6)),
        ],
        compiler_params=pltpu.CompilerParams(
            collective_id=0, has_side_effects=True, vmem_limit_bytes=60 << 20
        ),
    )(queries, keys, values, doc_lengths, out_weight)


def solution(mesh):
    in_specs = (P("ctx", "tp"), P("ctx", "tp"), P("ctx", "tp"), P(), P("tp", None))
    out_specs = P("ctx", "tp")
    return jax.shard_map(local, mesh=mesh, in_specs=in_specs, out_specs=out_specs, check_vma=False)
```

```python
import functools
import math

import jax
import jax.numpy as jnp
from jax import lax
from jax.experimental import pallas as pl
from jax.experimental.pallas import tpu as pltpu
from jax.sharding import PartitionSpec as P

MESH = pl.DeviceIdType.MESH
HEAD = 128
GROUP = 8
ROWS = 384
CHUNK = 512
NY, NZ, NX, NK = 4, 8, 4, 2
WIDE = 640
COLS = GROUP * ROWS
TILES = 3
TILE = ROWS // TILES
SPAN = GROUP * TILE
SCALE = math.log2(math.e) / math.sqrt(HEAD)
BIG = 262144.0
LOW = -1e30

SIZES = (2, 4, 4, 4, 4)
ORDER = (
    (7, 8, 1, 17, 18, 6, 5, 15, 2, 16, 9, 4, 3, 13, 14, 11, 10, 12),
    (1, 7, 8, 9, 18, 6, 5, 15, 2, 16, 17, 4, 3, 13, 14, 11, 10, 12),
    (1, 2, 7, 8, 9, 6, 5, 15, 10, 16, 17, 4, 3, 13, 14, 11, 18, 12),
    (1, 2, 7, 8, 9, 3, 6, 5, 15, 10, 16, 17, 4, 11, 13, 14, 18, 12),
    (1, 2, 7, 8, 9, 3, 6, 5, 15, 10, 16, 17, 12, 4, 11, 13, 14, 18),
    (1, 2, 7, 8, 9, 3, 6, 13, 15, 10, 16, 17, 12, 4, 11, 14, 18, 5),
    (1, 2, 7, 8, 9, 3, 14, 13, 6, 15, 10, 16, 17, 12, 4, 11, 18, 5),
    (1, 2, 15, 7, 8, 9, 3, 14, 13, 6, 10, 16, 17, 12, 4, 11, 18, 5),
)
TICKS = (
    (
        (1, 0, 0, 0, 7, 255), (1, 2, 0, 1, 0, 255), (1, 3, 0, 3, 0, 255), (1, 1, 1, 0, 1, 255),
        (1, 0, 1, 0, 7, 255), (1, 2, 1, 1, 0, 255), (1, 1, 0, 0, 1, 3),
    ),
    (
        (0, 0, 0, 7, 255), (1, 0, 0, 0, 6, 255), (1, 2, 0, 1, 7, 255), (1, 3, 0, 3, 7, 255),
        (0, 0, 1, 0, 255), (1, 1, 0, 1, 1, 255), (0, 0, 3, 0, 255), (1, 3, 0, 2, 0, 255), (0, 1, 0, 1, 255),
        (1, 2, 1, 1, 1, 255), (1, 1, 1, 0, 2, 129), (0, 1, 0, 7, 255), (1, 0, 1, 0, 6, 255),
        (1, 2, 1, 1, 7, 255), (1, 3, 1, 3, 7, 1), (0, 0, 0, 6, 255), (1, 0, 0, 0, 5, 255),
        (1, 3, 0, 3, 6, 255), (0, 0, 1, 1, 255), (1, 1, 0, 1, 2, 255), (0, 0, 2, 0, 255),
        (1, 1, 0, 2, 1, 254), (0, 1, 0, 6, 255), (1, 0, 1, 0, 5, 255), (1, 3, 1, 3, 6, 3), (0, 1, 1, 0, 255),
        (1, 2, 1, 2, 0, 255), (0, 1, 1, 1, 255), (1, 1, 1, 1, 2, 255), (1, 2, 1, 2, 1, 127),
        (0, 0, 0, 5, 255), (1, 0, 0, 0, 4, 120), (1, 3, 0, 3, 5, 135), (1, 2, 0, 1, 5, 255),
        (0, 0, 1, 2, 255), (1, 1, 0, 1, 3, 255), (0, 0, 1, 7, 255), (1, 0, 0, 1, 6, 255), (0, 0, 2, 1, 127),
        (1, 1, 0, 2, 2, 126), (0, 0, 3, 7, 255), (1, 3, 0, 2, 7, 255),
    ),
    (
        (0, 0, 0, 1, 129), (1, 1, 0, 0, 2, 129), (0, 0, 3, 6, 255), (1, 3, 0, 2, 6, 255), (0, 1, 1, 7, 255),
        (1, 0, 1, 1, 6, 255), (0, 1, 0, 5, 255), (1, 0, 1, 0, 4, 120), (1, 2, 1, 1, 5, 255),
        (0, 1, 1, 2, 255), (1, 1, 1, 1, 3, 255), (0, 1, 3, 6, 3), (0, 1, 3, 7, 1),
    ),
    (
        (0, 0, 0, 4, 240), (1, 0, 0, 0, 3, 112), (0, 0, 3, 5, 135), (1, 3, 0, 2, 5, 135), (0, 0, 2, 2, 63),
        (0, 0, 0, 2, 192), (0, 0, 1, 3, 255), (1, 1, 0, 1, 4, 255), (1, 2, 0, 2, 3, 31), (0, 1, 0, 2, 192),
        (0, 1, 1, 3, 255), (1, 2, 1, 2, 3, 31), (1, 1, 1, 1, 4, 255), (0, 1, 1, 6, 255), (1, 2, 1, 2, 6, 255),
        (0, 1, 2, 0, 255), (1, 0, 1, 2, 7, 255), (0, 1, 2, 1, 127), (1, 1, 1, 2, 2, 126), (0, 0, 1, 6, 255),
    ),
    (
        (0, 0, 2, 5, 135), (1, 0, 0, 2, 4, 135), (0, 1, 2, 3, 31), (1, 1, 1, 2, 4, 30), (0, 0, 1, 5, 255),
        (0, 1, 0, 4, 240), (1, 0, 1, 0, 3, 112), (0, 1, 1, 4, 255), (0, 1, 1, 5, 255), (1, 2, 1, 2, 5, 7),
        (0, 1, 2, 7, 255), (0, 0, 1, 4, 255), (0, 0, 2, 3, 31), (0, 0, 2, 7, 255),
    ),
    (
        (0, 1, 2, 4, 15), (0, 1, 2, 6, 255), (0, 1, 0, 3, 224), (0, 1, 2, 2, 63), (0, 1, 2, 5, 7),
        (0, 0, 0, 3, 224), (0, 0, 2, 4, 15), (0, 0, 2, 6, 255),
    ),
)
MESSAGES = tuple(item[1:] for tick in TICKS for item in tick if item[0] == 1)


def pick(index, numbers):
    value = jnp.int32(numbers[0])
    for at, number in enumerate(numbers[1:], 1):
        value = jnp.where(index == at, jnp.int32(number), value)
    return value


def kernel(
    q_ref, k_ref, v_ref, len_ref, w_ref, out_ref,
    q_own, qt, kv, acc, top, qpos, firsts, lasts, wts, att, far, near_r, near_l, mid_l, mid_r, in_l, in_r, mine,
    q_sem, kv_send, kv_recv, w_local, w_send, w_recv, a_send, a_recv, x_send, x_recv,
):
    ctx, tp = lax.axis_index("ctx"), lax.axis_index("tp")
    y, z = ctx // NZ, lax.rem(ctx, NZ)
    x, core = tp // NK, lax.rem(tp, NK)
    z_next = (y * NZ + lax.rem(z + 1, NZ), tp)
    z_back = (y * NZ + lax.rem(z + NZ - 1, NZ), tp)
    y_next = (lax.rem(y + 1, NY) * NZ + z, tp)
    y_back = (lax.rem(y + NY - 1, NY) * NZ + z, tp)
    x_next = (ctx, lax.rem(x + 1, NX) * NK + core)
    x_back = (ctx, lax.rem(x + NX - 1, NX) * NK + core)
    other = (ctx, x * NK + 1 - core)
    links = (z_next, z_back, y_next, y_back)
    shift = ((0, 1), (0, -1), (-1, 0), (1, 0))

    q_copy = pltpu.make_async_copy(q_ref, q_own, q_sem)
    q_copy.start()
    barrier = pltpu.get_barrier_semaphore()
    for device in links + (x_next, x_back, other):
        pl.semaphore_signal(barrier, inc=1, device_id=device, device_id_type=MESH)

    values_t = v_ref[...].astype(jnp.float32).T.astype(jnp.bfloat16)
    for c in range(3):
        kv[0, z, c, 0:HEAD, :] = k_ref[c * HEAD:(c + 1) * HEAD, :]
        kv[0, z, c, HEAD:, :] = values_t[:, c * HEAD:(c + 1) * HEAD]

    def message(link, part, row, column):
        piece = pl.ds(0, 1) if part == 0 else pl.ds(1, 2)
        dy, dz = shift[link]
        held = (row + dy) % NY
        col = lax.rem(z + (column + dz) + 2 * NZ, NZ)
        return pltpu.make_async_remote_copy(
            src_ref=kv.at[held, col, piece],
            dst_ref=kv.at[row, col, piece],
            send_sem=kv_send.at[part, row, column],
            recv_sem=kv_recv.at[part, row, column],
            device_id=links[link],
            device_id_type=MESH,
        )

    def arrival(part, row, column):
        piece = pl.ds(0, 1) if part == 0 else pl.ds(1, 2)
        slot = kv.at[row, lax.rem(z + column, NZ), piece]
        return pltpu.make_async_remote_copy(
            src_ref=slot,
            dst_ref=slot,
            send_sem=kv_send.at[part, row, column],
            recv_sem=kv_recv.at[part, row, column],
            device_id=z_next,
            device_id_type=MESH,
        )

    def where(mask, run):
        if mask == (1 << NZ) - 1:
            run()
            return
        within = None
        for first in range(NZ):
            if mask >> first & 1 and not (first and mask >> (first - 1) & 1):
                last = first
                while mask >> (last + 1) & 1:
                    last += 1
                here = (z >= first) & (z <= last)
                within = here if within is None else within | here
        pl.when(within)(run)

    def act(item):
        if item[0] == 0:
            where(item[-1], lambda: arrival(*item[1:-1]).wait_recv())
        else:
            where(item[-1], lambda: message(*item[1:-1]).start())

    pl.semaphore_wait(barrier, 7)
    for item in TICKS[0]:
        act(item)

    def weight_columns(xx, half):
        return pl.ds(pl.multiple_of(xx * (2 * WIDE) + half * WIDE, HEAD), WIDE)

    targets = [lax.rem(x + ahead, NX) for ahead in (2, 1, 3, 0)]

    def weight_keep(at):
        return pltpu.make_async_copy(
            w_ref.at[:, weight_columns(targets[at], core)], wts.at[core, :, pl.ds(at * WIDE, WIDE)], w_local.at[at]
        )

    def weight_give(at):
        return pltpu.make_async_remote_copy(
            src_ref=w_ref.at[:, weight_columns(targets[at], 1 - core)],
            dst_ref=wts.at[core, :, pl.ds(at * WIDE, WIDE)],
            send_sem=w_send.at[at],
            recv_sem=w_recv.at[at],
            device_id=other,
            device_id_type=MESH,
        )

    for xx in range(NX):
        weight_keep(xx).start()
        weight_give(xx).start()

    lane = lax.broadcasted_iota(jnp.int32, (8, HEAD), 1)
    sub = lax.broadcasted_iota(jnp.int32, (HEAD, ROWS), 0)
    first_l = jnp.where(lane == HEAD - 1, -(1 << 30), 0)
    last_l = jnp.zeros_like(lane)
    first_s, last_s = jnp.zeros_like(sub), jnp.zeros_like(sub)
    begin = jnp.int32(0)
    for d in range(24):
        end = begin + len_ref[d]
        first_l, last_l = jnp.where(lane == d, begin, first_l), jnp.where(lane == d, end, last_l)
        first_s, last_s = jnp.where(sub == d, begin, first_s), jnp.where(sub == d, end, last_s)
        begin = end
    firsts[...] = first_l
    lasts[...] = last_l
    own = ctx * ROWS + lax.broadcasted_iota(jnp.int32, (HEAD, ROWS), 1)
    apart = jnp.where((own >= first_s) & (own < last_s), 0.0, -BIG).astype(jnp.bfloat16)
    q_copy.wait()
    for h in range(GROUP):
        turned = q_own[:, h * HEAD:(h + 1) * HEAD].astype(jnp.float32).T.astype(jnp.bfloat16)
        for t in range(TILES):
            span = slice(t * SPAN + h * TILE, t * SPAN + (h + 1) * TILE)
            rows = slice(t * TILE, (t + 1) * TILE)
            qt[0:HEAD, span] = turned[:, rows]
            qt[HEAD:, span] = apart[:, rows]
            qpos[:, span] = own[0:8, rows]
    top[...] = jnp.full_like(top, LOW)
    acc[...] = jnp.zeros_like(acc)

    def block(delta):
        row = (delta - z + NZ - 1) // NZ
        col = lax.rem(z - delta + 3 * NZ, NZ)
        held = kv[row, col]
        pos = (ctx - delta) * ROWS + lax.broadcasted_iota(jnp.int32, (ROWS, HEAD), 0)
        same = jnp.where((pos >= firsts[0:1, :]) & (pos < lasts[0:1, :]), 1.0, 0.0).astype(jnp.bfloat16)
        keys = jnp.concatenate([held[c, 0:HEAD] for c in range(3)], axis=0)
        vals = jnp.concatenate([held[c, HEAD:] for c in range(3)], axis=1)
        return jnp.concatenate([keys, same], axis=1), vals

    def attend(deltas, causal, base, steps):
        parts = [block(delta) for delta in deltas]
        keys = jnp.concatenate([part[0] for part in parts], axis=0)
        vals = jnp.concatenate([part[1] for part in parts], axis=1)
        count = keys.shape[0]
        vals = jnp.concatenate([vals, jnp.ones((16, count), jnp.bfloat16)], axis=0)

        def span_of(j):
            if isinstance(base, int):
                return slice(base + j * CHUNK, base + (j + 1) * CHUNK)
            return pl.ds(pl.multiple_of(base + j * CHUNK, CHUNK), CHUNK)

        def score(j):
            span = span_of(j)
            got = jnp.dot(keys, qt[:, span], preferred_element_type=jnp.float32)
            if causal:
                pos = (ctx - deltas[0]) * ROWS + lax.broadcasted_iota(jnp.int32, (count, CHUNK), 0)
                got = jnp.where(pos <= qpos[0:1, span], got, -BIG)
            return got

        def soften(j, got):
            span = span_of(j)
            old = top[0:1, span]
            new = jnp.maximum(old, jnp.max(got, axis=0, keepdims=True))
            top[0:1, span] = new
            return jnp.exp2((got - new) * SCALE).astype(jnp.bfloat16), jnp.exp2((old - new) * SCALE)

        def gather(j, weights, fade):
            span = span_of(j)
            acc[:, span] = acc[:, span] * fade + jnp.dot(vals, weights, preferred_element_type=jnp.float32)

        got, held = score(0), None
        for j in range(steps):
            ahead = score(j + 1) if j + 1 < steps else None
            soft = soften(j, got)
            if held is not None:
                gather(j - 1, *held)
            got, held = ahead, soft
        gather(steps - 1, *held)

    order = [pick(z, [row[at] for row in ORDER]) for at in range(len(ORDER[0]))]
    groups, at = [[jnp.int32(0)]], 0
    for size in SIZES:
        groups.append(order[at:at + size])
        at += size
    last = groups.pop()
    sizes = [len(group) for group in groups]

    def least(deltas):
        return functools.reduce(jnp.minimum, deltas)

    def step(i, carry):
        for at in range(1, len(groups)):
            @pl.when(i == at)
            def _(at=at):
                for item in TICKS[at]:
                    act(item)

        for size in sorted(set(sizes)):
            deltas = []
            for slot in range(size):
                value = groups[0][0]
                for at, group in enumerate(groups):
                    if len(group) == size:
                        value = jnp.where(i == at, group[slot], value)
                deltas.append(value)
            now = functools.reduce(jnp.logical_or, [i == at for at in range(len(groups)) if sizes[at] == size])

            @pl.when(now & (ctx >= least(deltas)))
            def _(deltas=tuple(deltas), size=size):
                attend(deltas, size == 1, 0, COLS // CHUNK)

        return carry

    lax.fori_loop(0, len(groups), step, 0)

    for item in TICKS[len(groups)]:
        act(item)
    for xx in range(NX):
        weight_keep(xx).wait()
        weight_give(xx).wait()

    half = TILE // 2

    def swap(t, part):
        held = att.at[core, t, :, pl.ds(part * GROUP * HEAD // 2, GROUP * HEAD // 2)]
        return pltpu.make_async_remote_copy(
            src_ref=held, dst_ref=held, send_sem=a_send.at[t, part], recv_sem=a_recv.at[t, part], device_id=other, device_id_type=MESH,
        )

    def along(t, at, src, dst, device):
        return pltpu.make_async_remote_copy(
            src_ref=src,
            dst_ref=dst,
            send_sem=x_send.at[t, at],
            recv_sem=x_recv.at[t, at],
            device_id=device,
            device_id_type=MESH,
        )

    lower, upper = pl.ds(0, half), pl.ds(half, half)

    def copies(t):
        return (
            along(t, 0, far.at[t, lower], mid_l.at[t], x_next),
            along(t, 1, far.at[t, upper], mid_r.at[t], x_back),
            along(t, 2, near_r.at[t, upper], in_l.at[t, upper], x_next),
            along(t, 3, near_l.at[t, lower], in_r.at[t, lower], x_back),
            along(t, 4, near_r.at[t, lower], in_l.at[t, lower], x_next),
            along(t, 5, near_l.at[t, upper], in_r.at[t, upper], x_back),
        )

    def pass_on(t):
        far_up, far_down, _, _, up, down = copies(t)
        far_up.wait_recv()
        near_r[t, 0:half] = (near_r[t, 0:half].astype(jnp.float32) + mid_l[t].astype(jnp.float32)).astype(jnp.bfloat16)
        up.start()
        far_down.wait_recv()
        near_l[t, half:] = (near_l[t, half:].astype(jnp.float32) + mid_r[t].astype(jnp.float32)).astype(jnp.bfloat16)
        down.start()

    def finish(t, carry):
        base = t * SPAN

        @pl.when(ctx >= least(last))
        def _():
            attend(tuple(last), False, base, SPAN // CHUNK)

        for h in range(GROUP):
            span = pl.ds(pl.multiple_of(base + h * TILE, TILE), TILE)
            rows = acc[0:HEAD, span] * (1.0 / acc[HEAD:HEAD + 1, span])
            att[core, t, :, h * HEAD:(h + 1) * HEAD] = rows.T.astype(jnp.bfloat16)
            if h % (GROUP // 2) == GROUP // 2 - 1:
                swap(t, h // (GROUP // 2)).start()

        @pl.when(t > 0)
        def _():
            pass_on(t - 1)

        def term(of, at):
            return jnp.dot(att[of, t], wts[of, :, 2 * at * WIDE:2 * (at + 1) * WIDE], preferred_element_type=jnp.float32)

        far_up, far_down, up, down, _, _ = copies(t)
        total = term(core, 0)
        for part in range(2):
            swap(t, part).wait()
        total += term(1 - core, 0)
        far[t] = total[:, 0:WIDE].astype(jnp.bfloat16)
        far_up.start()
        far_down.start()
        near_r[t] = total[:, WIDE:].astype(jnp.bfloat16)
        total = term(core, 1) + term(1 - core, 1)
        near_l[t] = total[:, 0:WIDE].astype(jnp.bfloat16)
        up.start()
        down.start()
        mine[t] = total[:, WIDE:]
        return carry

    lax.fori_loop(0, TILES, finish, 0)

    def add_up(t):
        for copy in copies(t)[2:]:
            copy.wait_recv()
        total = mine[t] + in_l[t].astype(jnp.float32) + in_r[t].astype(jnp.float32)
        out_ref[t * TILE:(t + 1) * TILE] = total.astype(jnp.bfloat16)

    for t in range(TILES - 2):
        add_up(t)
    pass_on(TILES - 1)
    for t in range(TILES - 2, TILES):
        add_up(t)
    for t in range(TILES):
        for copy in copies(t):
            copy.wait_send()
    for item in MESSAGES:
        where(item[-1], lambda item=item: message(*item[:-1]).wait_send())


def local(queries, keys, values, doc_lengths, out_weight):
    vmem = pl.BlockSpec(memory_space=pltpu.VMEM)
    bf16, f32 = jnp.bfloat16, jnp.float32
    dma = pltpu.SemaphoreType.DMA
    return pl.pallas_call(
        kernel,
        out_shape=jax.ShapeDtypeStruct((ROWS, WIDE), bf16),
        in_specs=[pl.BlockSpec(memory_space=pl.ANY), vmem, vmem, pl.BlockSpec(memory_space=pltpu.SMEM), pl.BlockSpec(memory_space=pl.ANY)],
        out_specs=vmem,
        scratch_shapes=[
            pltpu.VMEM((ROWS, GROUP * HEAD), bf16),
            pltpu.VMEM((2 * HEAD, COLS), bf16),
            pltpu.VMEM((NY, NZ, 3, 2 * HEAD, HEAD), bf16),
            pltpu.VMEM((HEAD + 16, COLS), f32),
            pltpu.VMEM((8, COLS), f32),
            pltpu.VMEM((8, COLS), jnp.int32),
            pltpu.VMEM((8, HEAD), jnp.int32),
            pltpu.VMEM((8, HEAD), jnp.int32),
            pltpu.VMEM((NK, GROUP * HEAD, NX * WIDE), bf16),
            pltpu.VMEM((NK, TILES, TILE, GROUP * HEAD), bf16),
            pltpu.VMEM((TILES, TILE, WIDE), bf16),
            pltpu.VMEM((TILES, TILE, WIDE), bf16),
            pltpu.VMEM((TILES, TILE, WIDE), bf16),
            pltpu.VMEM((TILES, TILE // 2, WIDE), bf16),
            pltpu.VMEM((TILES, TILE // 2, WIDE), bf16),
            pltpu.VMEM((TILES, TILE, WIDE), bf16),
            pltpu.VMEM((TILES, TILE, WIDE), bf16),
            pltpu.VMEM((TILES, TILE, WIDE), f32),
            dma,
            dma((2, NY, NZ)),
            dma((2, NY, NZ)),
            dma((NX,)),
            dma((NX,)),
            dma((NX,)),
            dma((TILES, 2)),
            dma((TILES, 2)),
            dma((TILES, 6)),
            dma((TILES, 6)),
        ],
        compiler_params=pltpu.CompilerParams(
            collective_id=0, has_side_effects=True, vmem_limit_bytes=60 << 20
        ),
    )(queries, keys, values, doc_lengths, out_weight)


def solution(mesh):
    in_specs = (P("ctx", "tp"), P("ctx", "tp"), P("ctx", "tp"), P(), P("tp", None))
    out_specs = P("ctx", "tp")
    return jax.shard_map(local, mesh=mesh, in_specs=in_specs, out_specs=out_specs, check_vma=False)
```
